128 devices in a mesh: dx: 16 (over x, z_lo, core), dy: 8 (over z_hi, y).
Axes of the slice: x: 4, y: 4, z: 4 (z_hi: 2, z_lo: 2; z = z_hi * 2 + z_lo), core: 2. Of those that a mesh axis runs over, the one named last changes fastest.
Arguments:
- events: float32 [16384, 512], P(('dx', 'dy')), may hold values from -16 to 16
- images: float32 [16384, 512], P(('dx', 'dy')), may hold values from -16 to 16
- log_scale: float32 [1], replicated, may hold values from 4.8 to 5.5
Outputs:
- event_grad: float32 [16384, 512], P(('dx', 'dy'))
- image_grad: float32 [16384, 512], P(('dx', 'dy'))
- pair_loss: float32 [1], replicated
- scale_grad: float32 [1], replicated
The draws below stay inside these ranges and needn't reach their ends.
All inputs are finite; a program needn't handle non-finite values.
Results may differ from the reference program's by a relative error of at most 0.0089.
Values may be sent and summed in bfloat16 or wider, within the bound.
A program may use at most 192 MiB of HBM per device.

```python
import jax
import jax.numpy as jnp
from jax import lax

EMBED = 512
ROWS_DEV = 128
PAIRS = 16384


def anchor_rows(key):
    stride = PAIRS // 8
    offset = jax.random.randint(jax.random.fold_in(key, 13), (), 0, stride - 2)
    return offset + jnp.arange(8, dtype=jnp.int32) * stride


def image_field(key):
    normal_base = jax.random.normal(jax.random.fold_in(key, 11), (PAIRS, EMBED), jnp.float32)
    field = normal_base
    anchors = anchor_rows(key)
    field = field.at[anchors + 1].set(field[anchors + 1])
    return (field, anchors)


def draw_images(key, part):
    field, anchors = image_field(key)
    return jnp.clip(field, -16.0, 16.0)


def draw_events(key, part):
    field, anchors = image_field(key)
    key = jax.random.fold_in(key, 4)
    noise_rows = jax.random.normal(key, (PAIRS, EMBED), jnp.float32)
    result = 0.1 * field + noise_rows
    result = result.at[anchors].set(result[anchors])
    result = result.at[anchors + 1].set(result[anchors + 1])
    return jnp.clip(result, -16.0, 16.0)


def setup_inputs(seed: int = 0) -> dict:
    key_of = jax.random.split(jax.random.key(seed), 4)
    events = draw_events(jax.random.fold_in(key_of[3], 71), 0)
    images = draw_images(jax.random.fold_in(key_of[3], 71), 0)
    log_scale = jnp.clip(jax.random.uniform(key_of[2], (1,), jnp.float32, 4.8, 5.5), 4.8, 5.5)
    return dict(events=events, images=images, log_scale=log_scale)


EPSILON = 1e-06

def normalize(field):
    inverse = lax.rsqrt(lax.optimization_barrier(jnp.sum(field * field, axis=1, keepdims=True)) + EPSILON)
    return (field * inverse, inverse)

def reference(events, images, log_scale):
    temper = jnp.exp(log_scale[0])
    unit_e, inv_e = normalize(events)
    unit_i, inv_i = normalize(images)
    half_e = unit_e.astype(jnp.bfloat16)
    half_i = unit_i.astype(jnp.bfloat16)
    blocks = PAIRS // ROWS_DEV
    event_blocks = half_e.reshape(blocks, ROWS_DEV, EMBED)

    def pass_one(carry, row_block):
        col_max, col_tot = carry
        logits = temper * jnp.dot(row_block, half_i.T, preferred_element_type=jnp.float32)
        lse_rows = jax.nn.logsumexp(logits, axis=1)
        new_max = jnp.maximum(col_max, lax.optimization_barrier(jnp.max(logits, axis=0)))
        col_tot = col_tot * jnp.exp(col_max - new_max) + lax.optimization_barrier(jnp.sum(jnp.exp(logits - new_max[None, :]), axis=0))
        return ((new_max, col_tot), lse_rows)
    start_max = jnp.full((PAIRS,), -jnp.inf, jnp.float32)
    start_tot = jnp.zeros((PAIRS,), jnp.float32)
    (col_max, col_tot), lse_blocks = lax.scan(pass_one, (start_max, start_tot), event_blocks)
    row_lse = lse_blocks.reshape(PAIRS)
    col_lse = col_max + jnp.log(col_tot)
    columns = jnp.arange(PAIRS, dtype=jnp.int32)

    def pass_two(carry, inputs):
        image_dir, scale_sum = carry
        row_block, lse_block, number = inputs
        logits = temper * jnp.dot(row_block, half_i.T, preferred_element_type=jnp.float32)
        row_ids = number * ROWS_DEV + jnp.arange(ROWS_DEV, dtype=jnp.int32)
        onehot = (row_ids[:, None] == columns[None, :]).astype(jnp.float32)
        gradient = 0.5 * jnp.exp(logits - lse_block[:, None]) + 0.5 * jnp.exp(logits - col_lse[None, :]) - onehot
        weight = (temper * gradient).astype(jnp.bfloat16)
        event_dir = jnp.dot(weight, half_i, preferred_element_type=jnp.float32)
        image_dir = image_dir + lax.dot_general(weight, row_block, (((0,), (0,)), ((), ())), preferred_element_type=jnp.float32)
        scale_sum = scale_sum + jnp.sum(gradient * logits)
        return ((image_dir, scale_sum), event_dir)
    numbers = jnp.arange(blocks, dtype=jnp.int32)
    start_dir = jnp.zeros((PAIRS, EMBED), jnp.float32)
    (image_dir, scale_sum), event_dirs = lax.scan(pass_two, (start_dir, jnp.zeros((), jnp.float32)), (event_blocks, lse_blocks, numbers))
    event_dir = event_dirs.reshape(PAIRS, EMBED)
    diagonal = temper * lax.optimization_barrier(jnp.sum(half_e.astype(jnp.float32) * half_i.astype(jnp.float32), axis=1))
    loss_sum = 0.5 * jnp.sum(row_lse - diagonal) + 0.5 * jnp.sum(col_lse - diagonal)
    event_grad = inv_e * (event_dir - unit_e * lax.optimization_barrier(jnp.sum(unit_e * event_dir, axis=1, keepdims=True)))
    image_grad = inv_i * (image_dir - unit_i * lax.optimization_barrier(jnp.sum(unit_i * image_dir, axis=1, keepdims=True)))
    pair_loss = (loss_sum / PAIRS).reshape(1)
    scale_grad = (scale_sum / PAIRS).reshape(1)
    return (event_grad, image_grad, pair_loss, scale_grad)
```

```python
import functools

import jax
import jax.numpy as jnp
from jax import lax
from jax.experimental import pallas as pl
from jax.experimental.pallas import tpu as pltpu
from jax.sharding import PartitionSpec as P

EPSILON = 1e-06
MESH = pl.DeviceIdType.MESH
LOG2E = 1.4426950408889634
LN2 = 0.6931471805599453
ROWS = 128
F32 = jnp.float32
BF16 = jnp.bfloat16


def gray(t):
    return t ^ (t >> 1)


def dot_t(a, b):
    return lax.dot_general(a, b, (((1,), (1,)), ((), ())), preferred_element_type=F32)


def dot(a, b):
    return lax.dot_general(a, b, (((1,), (0,)), ((), ())), preferred_element_type=F32)


def kernel(
    X,
    Y,
    ev_ref,
    im_ref,
    ls_ref,
    eg_ref,
    ig_ref,
    loss_ref,
    sg_ref,
    e_all,
    et_all,
    i_all,
    lg,
    wt,
    rm,
    rs,
    rl,
    cl,
    row_recv,
    col_a,
    col_b,
    col_recv,
    sib_send,
    sib_recv,
    own_part,
    di_send,
    di_recv,
    de_send,
    de_recv,
    sc1_recv,
    sc2_recv,
    acc,
    e_ss,
    e_rs,
    i_ss,
    i_rs,
    f_ss,
    f_rs,
    r_ss,
    r_rs,
    c_ss,
    c_rs,
    s_ss,
    s_rs,
    di_ss,
    di_rs,
    de_ss,
    de_rs,
    a_ss,
    a_rs,
    b_ss,
    b_rs,
):
    NB, NJ = 2 * Y, 2 * X
    D = ev_ref.shape[1]
    dx, dy = lax.axis_index("dx"), lax.axis_index("dy")
    core, zl, x = dx % 2, (dx // 2) % 2, dx // 4
    y, zh = dy % Y, dy // Y
    own_b, own_j = y * 2 + zl, x * 2 + zh

    def row_member(k):
        oy, f = gray(k // 2) % Y, k % 2
        ty, tzl = (y + oy) % Y, zl ^ f
        return ((x * 2 + tzl) * 2 + core, zh * Y + ty), ty * 2 + tzl

    def col_member(k, r):
        ox, f = gray(k // 2) % X, k % 2
        tx, tzl, tzh = (x + ox) % X, zl ^ f, zh ^ f
        return ((tx * 2 + tzl) * 2 + (core ^ r), tzh * Y + y), tx * 2 + tzh

    def remote(src, dst, ss, rsem, device):
        return pltpu.make_async_remote_copy(
            src_ref=src,
            dst_ref=dst,
            send_sem=ss,
            recv_sem=rsem,
            device_id=device,
            device_id_type=MESH,
        )

    barrier = pltpu.get_barrier_semaphore()
    for k in range(1, NB):
        pl.semaphore_signal(barrier, inc=1, device_id=row_member(k)[0], device_id_type=MESH)
    for r in range(2):
        for k in range(1 - r, NJ):
            pl.semaphore_signal(
                barrier, inc=1, device_id=col_member(k, r)[0], device_id_type=MESH
            )

    def inverse(ref):
        v = ref[...]
        return lax.rsqrt(jnp.sum(v * v, axis=1, keepdims=True) + EPSILON)

    inv_e, inv_i = inverse(ev_ref), inverse(im_ref)
    e_all[own_b] = (ev_ref[...] * inv_e).astype(BF16)
    i_all[own_j, 0:ROWS] = (im_ref[...] * inv_i).astype(BF16)

    pl.semaphore_wait(barrier, (NB - 1) + (2 * NJ - 1))

    def e_copy(k, slot):
        device, other = row_member(k)
        return remote(e_all.at[slot], e_all.at[slot], e_ss.at[k], e_rs.at[slot], device)

    def i_copy(k, slot):
        device, _ = col_member(k, 0)
        block = i_all.at[slot, pl.ds(0, ROWS)]
        return remote(block, block, i_ss.at[k], i_rs.at[slot], device)

    def f_copy(slot):
        device, _ = col_member(0, 1)
        return remote(
            i_all.at[slot, pl.ds(0, ROWS)],
            i_all.at[slot, pl.ds(ROWS, ROWS)],
            f_ss.at[slot],
            f_rs.at[slot],
            device,
        )

    f_copy(own_j).start()
    for k in range(1, max(NB, NJ)):
        if k < NJ:
            i_copy(k, own_j).start()
        if k < NB:
            e_copy(k, own_b).start()

    scale = jnp.exp(jnp.full((1, ROWS), ls_ref[0], F32))
    scale2 = jnp.concatenate([scale, scale], axis=1)
    to_base2 = scale2 * LOG2E
    rm[...] = jnp.full(rm.shape, -1e30, F32)
    rs[...] = jnp.zeros(rs.shape, F32)

    def e_arrive(k, _):
        _, b = row_member(k)

        @pl.when(k > 0)
        def _():
            e_copy(0, b).wait_recv()

        et_all[:, pl.ds(pl.multiple_of(b * ROWS, ROWS), ROWS)] = e_all[b].T
        return 0

    lax.fori_loop(0, NB, e_arrive, 0)

    eye = lax.broadcasted_iota(jnp.int32, (ROWS, ROWS), 0) == lax.broadcasted_iota(
        jnp.int32, (ROWS, ROWS), 1
    )

    def to_lanes(column):
        return jnp.sum(jnp.where(eye, column, 0.0), axis=0, keepdims=True)

    def to_rows(lanes):
        return jnp.sum(jnp.where(eye, lanes, 0.0), axis=1, keepdims=True)

    def halves(v):
        return v[:, :ROWS], v[:, ROWS:]

    def fold(v, op):
        return op(v.reshape(v.shape[0] // 8, 8, v.shape[1]), axis=0)

    def one_chunk(k, _):
        _, j = col_member(k, 0)

        @pl.when(k + 1 < NJ)
        def _():
            _, nxt = col_member(k + 1, 0)
            i_copy(0, nxt).wait_recv()
            f_copy(nxt).start()

        f_copy(j).wait_recv()
        lg[j] = dot_t(e_all[...].reshape(NB * ROWS, D), i_all[j]) * to_base2

        def first(b, top):
            at = pl.ds(pl.multiple_of(b * ROWS, ROWS), ROWS)
            v = lg[j, at]
            v0, v1 = halves(v)
            old = rm[at]
            new = jnp.maximum(old, jnp.maximum(v0, v1))
            rs[at] = rs[at] * jnp.exp2(old - new) + jnp.exp2(v0 - new) + jnp.exp2(v1 - new)
            rm[at] = new
            return jnp.maximum(top, fold(v, jnp.max))

        top = lax.fori_loop(0, NB, first, jnp.full((8, 2 * ROWS), -1e30, F32))
        top = jnp.max(top, axis=0, keepdims=True)

        def second(b, tot):
            at = pl.ds(pl.multiple_of(b * ROWS, ROWS), ROWS)
            return tot + fold(jnp.exp2(lg[j, at] - top), jnp.sum)

        tot = lax.fori_loop(0, NB, second, jnp.zeros((8, 2 * ROWS), F32))
        own, sib = halves(top + jnp.log2(jnp.sum(tot, axis=0, keepdims=True)))
        col_a[pl.ds(2 * j, 1)] = own
        col_a[pl.ds(2 * j + 1, 1)] = sib
        col_b[pl.ds(2 * j, 1)] = sib
        col_b[pl.ds(2 * j + 1, 1)] = own
        return 0

    lax.fori_loop(0, NJ, one_chunk, 0)

    def c_copy(k, r, slot):
        device, _ = col_member(k, r)
        return remote(
            col_b if r else col_a,
            col_recv.at[slot],
            c_ss.at[r, k],
            c_rs.at[slot],
            device,
        )

    for r in range(2):
        for k in range(1 - r, NJ):
            c_copy(k, r, own_j * 2 + r).start()

    def row_done(b, _):
        at = pl.ds(pl.multiple_of(b * ROWS, ROWS), ROWS)
        v = rm[at]
        top = jnp.max(v, axis=1, keepdims=True)
        tot = jnp.sum(rs[at] * jnp.exp2(v - top), axis=1, keepdims=True)
        row_recv[own_b, pl.ds(b, 1)] = to_lanes(top + jnp.log2(tot))
        return 0

    lax.fori_loop(0, NB, row_done, 0)

    def r_copy(k, slot):
        device, _ = row_member(k)
        return remote(row_recv.at[slot], row_recv.at[slot], r_ss.at[k], r_rs.at[slot], device)

    for k in range(1, NB):
        r_copy(k, own_b).start()
    col_recv[own_j * 2] = col_a[...]
    for r in range(2):
        for k in range(1 - r, NJ):
            _, j = col_member(k, r)
            c_copy(0, r, j * 2 + r).wait_recv()
    v = col_recv[...]
    top = jnp.max(v, axis=0)
    cl[...] = top + jnp.log2(jnp.sum(jnp.exp2(v - top[None]), axis=0))
    for k in range(1, NB):
        _, b = row_member(k)
        r_copy(0, b).wait_recv()
    v = row_recv[...]
    top = jnp.max(v, axis=0)
    row_lse = top + jnp.log2(jnp.sum(jnp.exp2(v - top[None]), axis=0))
    for b in range(NB):
        rl[b] = jnp.broadcast_to(to_rows(row_lse[b : b + 1]), (ROWS, ROWS))

    half_scale = 0.5 * scale2
    acc[...] = jnp.zeros(acc.shape, F32)

    def s_copy(j):
        device, _ = col_member(0, 1)
        return remote(sib_send.at[j], sib_recv.at[j], s_ss.at[j], s_rs.at[j], device)

    def di_copy(k, j, slot):
        device, _ = col_member(k, 0)
        return remote(di_send.at[j], di_recv.at[slot], di_ss.at[k], di_rs.at[slot], device)

    def pass_on(k):
        device, j = col_member(k, 0)
        s_copy(j).wait_recv()
        total = own_part[j] + sib_recv[j].astype(F32)

        @pl.when(k > 0)
        def _():
            di_send[j] = total.astype(BF16)
            di_copy(k, j, own_j).start()

        @pl.when(k == 0)
        def _():
            di_recv[j] = total.astype(BF16)

    own_at = pl.ds(pl.multiple_of(own_b * ROWS, ROWS), ROWS)

    def weights(t, _):
        k = NJ - 1 - t
        _, j = col_member(k, 0)
        lse0, lse1 = cl[pl.ds(2 * j, 1)], cl[pl.ds(2 * j + 1, 1)]

        def block(b, _):
            at = pl.ds(pl.multiple_of(b * ROWS, ROWS), ROWS)
            v0, v1 = halves(lg[j, at])
            lse = rl[b]
            g0 = jnp.exp2(v0 - lse) + jnp.exp2(v0 - lse0)
            g1 = jnp.exp2(v1 - lse) + jnp.exp2(v1 - lse1)
            acc[...] += fold(g0 * v0 + g1 * v1, jnp.sum)
            wt[j, at] = (jnp.concatenate([g0, g1], axis=1) * half_scale).astype(BF16)
            return 0

        lax.fori_loop(0, NB, block, 0)

        @pl.when(k == 0)
        def _():
            v0 = lg[own_j, own_at, pl.ds(0, ROWS)]
            g0 = jnp.exp2(v0 - rl[own_b]) + jnp.exp2(v0 - lse0)
            wt[own_j, own_at, pl.ds(0, ROWS)] = (
                jnp.where(eye, g0 - 2.0, g0) * half_scale[:, :ROWS]
            ).astype(BF16)

        part = dot(et_all[...], wt[j])
        own_part[j] = part[:, :ROWS]
        sib_send[j] = part[:, ROWS:].astype(BF16)
        s_copy(j).start()

        @pl.when(t > 0)
        def _():
            pass_on(k + 1)

        return 0

    lax.fori_loop(0, NJ, weights, 0)

    diagonal = jnp.sum(
        jnp.where(eye, lg[own_j, own_at, pl.ds(0, ROWS)], 0.0), axis=0, keepdims=True
    )
    own_row_lse = to_lanes(rl[own_b])
    loss = 0.5 * (own_row_lse + cl[pl.ds(2 * own_j, 1)]) - diagonal
    grad = 0.5 * jnp.sum(acc[...], axis=0, keepdims=True) - diagonal
    rows8 = lax.broadcasted_iota(jnp.int32, (8, ROWS), 0)
    sc1_recv[own_b] = jnp.where(rows8 == 0, loss, jnp.where(rows8 == 1, grad, 0.0)) * LN2

    def a_copy(k, slot):
        device, _ = row_member(k)
        return remote(sc1_recv.at[slot], sc1_recv.at[slot], a_ss.at[k], a_rs.at[slot], device)

    for k in range(1, NB):
        a_copy(k, own_b).start()

    def de_copy(k, b, slot):
        device, _ = row_member(k)
        return remote(de_send.at[b], de_recv.at[slot], de_ss.at[k], de_rs.at[slot], device)

    def directions(t, _):
        base = Y - 1 - t
        _, b0 = row_member(2 * base)
        ty = b0 // 2
        at = pl.ds(pl.multiple_of(ty * 2 * ROWS, 2 * ROWS), 2 * ROWS)
        total = dot(wt[0, at], i_all[0])
        for j in range(1, NJ):
            total = total + dot(wt[j, at], i_all[j])
        total = total.astype(BF16).reshape(2, ROWS, D)
        de_send[2 * ty] = total[0]
        de_send[2 * ty + 1] = total[1]
        for f in range(2):
            k = 2 * base + f
            _, b = row_member(k)

            @pl.when(k > 0)
            def _():
                de_copy(k, b, own_b).start()

        return 0

    lax.fori_loop(0, Y, directions, 0)
    pass_on(0)

    for k in range(1, NB):
        _, b = row_member(k)
        a_copy(0, b).wait_recv()
    sc2_recv[own_j * 2] = jnp.sum(sc1_recv[...], axis=0)

    def b_copy(k, r, slot):
        device, _ = col_member(k, r)
        return remote(
            sc2_recv.at[own_j * 2], sc2_recv.at[slot], b_ss.at[r, k], b_rs.at[slot], device
        )

    for r in range(2):
        for k in range(1 - r, NJ):
            b_copy(k, r, own_j * 2 + r).start()

    def finish(field_ref, inv, direction, out_ref):
        unit = field_ref[...] * inv
        out_ref[...] = inv * (
            direction - unit * jnp.sum(unit * direction, axis=1, keepdims=True)
        )

    for k in range(1, NJ):
        _, j = col_member(k, 0)
        di_copy(0, j, j).wait_recv()
    total = di_recv[0].astype(F32)
    for j in range(1, NJ):
        total = total + di_recv[j].astype(F32)
    finish(im_ref, inv_i, total.T, ig_ref)

    de_recv[own_b] = de_send[own_b]
    for k in range(1, NB):
        _, b = row_member(k)
        de_copy(0, b, b).wait_recv()
    total = de_recv[0].astype(F32)
    for b in range(1, NB):
        total = total + de_recv[b].astype(F32)
    finish(ev_ref, inv_e, total, eg_ref)

    for r in range(2):
        for k in range(1 - r, NJ):
            _, j = col_member(k, r)
            b_copy(0, r, j * 2 + r).wait_recv()
    both = jnp.sum(sc2_recv[...], axis=0) * (1.0 / (NB * NJ * 2 * ROWS))
    loss_ref[0] = jnp.sum(both[0:1])
    sg_ref[0] = jnp.sum(both[1:2])

    for k in range(1, NB):
        e_copy(k, own_b).wait_send()
        r_copy(k, own_b).wait_send()
        a_copy(k, own_b).wait_send()
        _, b = row_member(k)
        de_copy(k, b, own_b).wait_send()
    for k in range(NJ):
        _, j = col_member(k, 0)
        f_copy(j).wait_send()
        s_copy(j).wait_send()
        if k > 0:
            i_copy(k, own_j).wait_send()
            di_copy(k, j, own_j).wait_send()
    for r in range(2):
        for k in range(1 - r, NJ):
            c_copy(k, r, own_j * 2 + r).wait_send()
            b_copy(k, r, own_j * 2 + r).wait_send()


def solution(mesh):
    X, Y = mesh.shape["dx"] // 4, mesh.shape["dy"] // 2
    NB, NJ = 2 * Y, 2 * X

    def on_device(events, images, log_scale):
        rows, D = events.shape
        dma = pltpu.SemaphoreType.DMA
        vmem = pl.BlockSpec(memory_space=pltpu.VMEM)
        smem = pl.BlockSpec(memory_space=pltpu.SMEM)
        block = jax.ShapeDtypeStruct((rows, D), F32)
        scalar = jax.ShapeDtypeStruct((1,), F32)
        V = pltpu.VMEM
        return pl.pallas_call(
            functools.partial(kernel, X, Y),
            out_shape=(block, block, scalar, scalar),
            in_specs=[vmem, vmem, smem],
            out_specs=(vmem, vmem, smem, smem),
            scratch_shapes=[
                V((NB, ROWS, D), BF16),
                V((D, NB * ROWS), BF16),
                V((NJ, 2 * ROWS, D), BF16),
                V((NJ, NB * ROWS, 2 * ROWS), F32),
                V((NJ, NB * ROWS, 2 * ROWS), BF16),
                V((NB * ROWS, ROWS), F32),
                V((NB * ROWS, ROWS), F32),
                V((NB, ROWS, ROWS), F32),
                V((2 * NJ, ROWS), F32),
                V((NB, NB, ROWS), F32),
                V((2 * NJ, ROWS), F32),
                V((2 * NJ, ROWS), F32),
                V((2 * NJ, 2 * NJ, ROWS), F32),
                V((NJ, D, ROWS), BF16),
                V((NJ, D, ROWS), BF16),
                V((NJ, D, ROWS), F32),
                V((NJ, D, ROWS), BF16),
                V((NJ, D, ROWS), BF16),
                V((NB, ROWS, D), BF16),
                V((NB, ROWS, D), BF16),
                V((NB, 8, ROWS), F32),
                V((2 * NJ, 8, ROWS), F32),
                V((8, ROWS), F32),
                dma((NB,)),
                dma((NB,)),
                dma((NJ,)),
                dma((NJ,)),
                dma((NJ,)),
                dma((NJ,)),
                dma((NB,)),
                dma((NB,)),
                dma((2, NJ)),
                dma((2 * NJ,)),
                dma((NJ,)),
                dma((NJ,)),
                dma((NJ,)),
                dma((NJ,)),
                dma((NB,)),
                dma((NB,)),
                dma((NB,)),
                dma((NB,)),
                dma((2, NJ)),
                dma((2 * NJ,)),
            ],
            compiler_params=pltpu.CompilerParams(
                collective_id=0,
                has_side_effects=True,
                vmem_limit_bytes=48 * 1024 * 1024,
            ),
        )(events, images, log_scale)

    return jax.shard_map(
        on_device,
        mesh=mesh,
        in_specs=(P(("dx", "dy"), None), P(("dx", "dy"), None), P()),
        out_specs=(P(("dx", "dy"), None), P(("dx", "dy"), None), P(), P()),
        check_vma=False,
    )
```

```python
import functools

import jax
import jax.numpy as jnp
from jax import lax
from jax.experimental import pallas as pl
from jax.experimental.pallas import tpu as pltpu
from jax.sharding import PartitionSpec as P

EPSILON = 1e-06
MESH = pl.DeviceIdType.MESH
LOG2E = 1.4426950408889634
LN2 = 0.6931471805599453
ROWS = 128
F32 = jnp.float32
BF16 = jnp.bfloat16


def gray(t):
    return t ^ (t >> 1)


def dot_t(a, b):
    return lax.dot_general(a, b, (((1,), (1,)), ((), ())), preferred_element_type=F32)


def dot(a, b):
    return lax.dot_general(a, b, (((1,), (0,)), ((), ())), preferred_element_type=F32)


def kernel(
    X,
    Y,
    ev_hbm,
    im_hbm,
    ls_hbm,
    grads_ref,
    sums_ref,
    ev_ref,
    im_ref,
    ls_ref,
    e_all,
    et_all,
    i_all,
    it_all,
    lg,
    wt,
    rm,
    rs,
    cm,
    cs,
    rl,
    cl,
    row_recv,
    col_a,
    col_b,
    col_recv,
    sib_send,
    sib_recv,
    own_part,
    di_send,
    di_recv,
    de_send,
    de_recv,
    sc1_recv,
    sc2_recv,
    in_s,
    e_ss,
    e_rs,
    i_ss,
    i_rs,
    f_ss,
    f_rs,
    r_ss,
    r_rs,
    c_ss,
    c_rs,
    s_ss,
    s_rs,
    di_ss,
    di_rs,
    de_ss,
    de_rs,
    a_ss,
    a_rs,
    b_ss,
    b_rs,
):
    NB, NJ = 2 * Y, 2 * X
    STEPS = max(X, Y)
    D = ev_ref.shape[1]
    PAIR, QUAD = 2 * ROWS, 4 * ROWS
    dx, dy = lax.axis_index("dx"), lax.axis_index("dy")
    core, zl, x = dx % 2, (dx // 2) % 2, dx // 4
    y, zh = dy % Y, dy // Y
    own_b, own_j = y * 2 + zl, x * 2 + zh

    def row_at(t):
        return (y + gray(t)) % Y

    def col_at(t):
        return (x + gray(t)) % X

    def row_member(k):
        ty, tzl = row_at(k // 2), zl ^ (k % 2)
        return ((x * 2 + tzl) * 2 + core, zh * Y + ty), ty * 2 + tzl

    def col_member(k, r):
        f = k % 2
        tx, tzl, tzh = col_at(k // 2), zl ^ f, zh ^ f
        return ((tx * 2 + tzl) * 2 + (core ^ r), tzh * Y + y), tx * 2 + tzh

    def remote(src, dst, ss, rsem, device):
        return pltpu.make_async_remote_copy(
            src_ref=src,
            dst_ref=dst,
            send_sem=ss,
            recv_sem=rsem,
            device_id=device,
            device_id_type=MESH,
        )

    loads = [
        pltpu.make_async_copy(ev_hbm, ev_ref, in_s.at[0]),
        pltpu.make_async_copy(im_hbm, im_ref, in_s.at[1]),
        pltpu.make_async_copy(ls_hbm, ls_ref, in_s.at[2]),
    ]
    for load in loads:
        load.start()
    barrier = pltpu.get_barrier_semaphore()
    for k in range(1, NB):
        pl.semaphore_signal(barrier, inc=1, device_id=row_member(k)[0], device_id_type=MESH)
    for r in range(2):
        for k in range(1 - r, NJ):
            pl.semaphore_signal(
                barrier, inc=1, device_id=col_member(k, r)[0], device_id_type=MESH
            )
    for load in loads:
        load.wait()

    def inverse(ref):
        v = ref[...]
        return lax.rsqrt(jnp.sum(v * v, axis=1, keepdims=True) + EPSILON)

    inv_e, inv_i = inverse(ev_ref), inverse(im_ref)
    e_all[own_b] = (ev_ref[...] * inv_e).astype(BF16)
    i_all[own_j, 0:ROWS] = (im_ref[...] * inv_i).astype(BF16)
    scale = jnp.exp(jnp.full((1, ROWS), ls_ref[0], F32))
    scale4 = jnp.concatenate([scale] * 4, axis=1)
    to_base2 = scale4 * LOG2E
    rm[...] = jnp.full(rm.shape, -1e30, F32)
    rs[...] = jnp.zeros(rs.shape, F32)
    cm[...] = jnp.full(cm.shape, -1e30, F32)
    cs[...] = jnp.zeros(cs.shape, F32)

    pl.semaphore_wait(barrier, (NB - 1) + (2 * NJ - 1))

    def e_copy(k, slot):
        device, _ = row_member(k)
        return remote(e_all.at[slot], e_all.at[slot], e_ss.at[k], e_rs.at[slot], device)

    def i_copy(k, slot):
        device, _ = col_member(k, 0)
        block = i_all.at[slot, pl.ds(0, ROWS)]
        return remote(block, block, i_ss.at[k], i_rs.at[slot], device)

    def f_copy(slot):
        device, _ = col_member(0, 1)
        return remote(
            i_all.at[slot, pl.ds(0, ROWS)],
            i_all.at[slot, pl.ds(ROWS, ROWS)],
            f_ss.at[slot],
            f_rs.at[slot],
            device,
        )

    order = [1, 2, 4, 3, 5, 6, 7]
    f_copy(own_j).start()
    for k in order:
        if k < NJ:
            i_copy(k, own_j).start()
        if k < NB:
            e_copy(k, own_b).start()

    eye = lax.broadcasted_iota(jnp.int32, (ROWS, ROWS), 0) == lax.broadcasted_iota(
        jnp.int32, (ROWS, ROWS), 1
    )

    def to_lanes(column):
        return jnp.sum(jnp.where(eye, column, 0.0), axis=0, keepdims=True)

    def to_rows(lanes):
        return jnp.sum(jnp.where(eye, lanes, 0.0), axis=1, keepdims=True)

    def lanes_of(v):
        return [v[:, ROWS * c : ROWS * (c + 1)] for c in range(v.shape[1] // ROWS)]

    def fold(v, op):
        return op(v.reshape(v.shape[0] // 8, 8, v.shape[1]), axis=0)

    def rows_of(ty):
        return pl.ds(pl.multiple_of(ty * PAIR, PAIR), PAIR)

    def tile(ty, tx):
        at = rows_of(ty)
        v = dot(e_all[pl.ds(2 * ty, 2)].reshape(PAIR, D), it_all[tx]) * to_base2
        lg[tx, at] = v
        parts = lanes_of(v)
        old = rm[at]
        new = functools.reduce(jnp.maximum, parts, old)
        rs[at] = functools.reduce(
            jnp.add, [jnp.exp2(p - new) for p in parts], rs[at] * jnp.exp2(old - new)
        )
        rm[at] = new
        old = cm[tx]
        new = jnp.maximum(old, fold(v, jnp.max))
        terms = jnp.exp2(v.reshape(PAIR // 8, 8, QUAD) - new[None])
        cs[tx] = cs[tx] * jnp.exp2(old - new) + jnp.sum(terms, axis=0)
        cm[tx] = new

    def images_arrive(t):
        for k in (2 * t, 2 * t + 1):
            if k > 0:
                _, j = col_member(k, 0)
                i_copy(0, j).wait_recv()
                f_copy(j).start()

    images_arrive(0)
    for t in range(STEPS):
        if t + 1 < X:
            images_arrive(t + 1)
        if t < Y:
            ty = row_at(t)
            for k in (2 * t, 2 * t + 1):
                if k > 0:
                    e_copy(0, row_member(k)[1]).wait_recv()
            et_all[:, rows_of(ty)] = e_all[pl.ds(2 * ty, 2)].reshape(PAIR, D).T
        if t < X:
            tx = col_at(t)
            for k in (2 * t, 2 * t + 1):
                f_copy(col_member(k, 0)[1]).wait_recv()
            it_all[tx] = i_all[pl.ds(2 * tx, 2)].reshape(QUAD, D).T
        for u in range(t + 1):
            if t < Y and u < X:
                tile(row_at(t), col_at(u))
            if u < t and u < Y and t < X:
                tile(row_at(u), col_at(t))

    def r_copy(k, slot):
        device, _ = row_member(k)
        return remote(row_recv.at[slot], row_recv.at[slot], r_ss.at[k], r_rs.at[slot], device)

    def c_copy(k, r, slot):
        device, _ = col_member(k, r)
        return remote(
            col_b if r else col_a,
            col_recv.at[slot],
            c_ss.at[r, k],
            c_rs.at[slot],
            device,
        )

    for b in range(NB):
        at = pl.ds(b * ROWS, ROWS)
        v = rm[at]
        top = jnp.max(v, axis=1, keepdims=True)
        tot = jnp.sum(rs[at] * jnp.exp2(v - top), axis=1, keepdims=True)
        row_recv[own_b, pl.ds(b, 1)] = to_lanes(top + jnp.log2(tot))
    for k in order:
        if k < NB:
            r_copy(k, own_b).start()
    for tx in range(X):
        top = jnp.max(cm[tx], axis=0, keepdims=True)
        tot = jnp.sum(cs[tx] * jnp.exp2(cm[tx] - top), axis=0, keepdims=True)
        for c, part in enumerate(lanes_of(top + jnp.log2(tot))):
            col_a[pl.ds(4 * tx + c, 1)] = part
            col_b[pl.ds(4 * tx + (c ^ 1), 1)] = part
    for r in range(2):
        for k in range(1 - r, NJ):
            c_copy(k, r, own_j * 2 + r).start()
    col_recv[own_j * 2] = col_a[...]
    for k in range(1, NB):
        e_copy(k, own_b).wait_send()
    for k in range(NJ):
        f_copy(col_member(k, 0)[1]).wait_send()
        if k > 0:
            i_copy(k, own_j).wait_send()
    for r in range(2):
        for k in range(1 - r, NJ):
            _, j = col_member(k, r)
            c_copy(0, r, j * 2 + r).wait_recv()
    v = col_recv[...]
    top = jnp.max(v, axis=0)
    v = top + jnp.log2(jnp.sum(jnp.exp2(v - top[None]), axis=0))
    for tx in range(X):
        cl[tx] = jnp.concatenate([v[4 * tx + c : 4 * tx + c + 1] for c in range(4)], axis=1)
    for k in range(1, NB):
        _, b = row_member(k)
        r_copy(0, b).wait_recv()
    v = row_recv[...]
    top = jnp.max(v, axis=0)
    row_lse = top + jnp.log2(jnp.sum(jnp.exp2(v - top[None]), axis=0))
    for b in range(NB):
        rl[pl.ds(b * ROWS, ROWS)] = jnp.broadcast_to(to_rows(row_lse[b : b + 1]), (ROWS, ROWS))

    half_scale = 0.5 * scale4

    def s_copy(j):
        device, _ = col_member(0, 1)
        return remote(sib_send.at[j], sib_recv.at[j], s_ss.at[j], s_rs.at[j], device)

    def di_copy(k, j, slot):
        device, _ = col_member(k, 0)
        return remote(di_send.at[j], di_recv.at[slot], di_ss.at[k], di_rs.at[slot], device)

    def de_copy(k, b, slot):
        device, _ = row_member(k)
        return remote(de_send.at[b], de_recv.at[slot], de_ss.at[k], de_rs.at[slot], device)

    own_at = pl.ds(pl.multiple_of(own_b * ROWS, ROWS), ROWS)
    own_cols = pl.ds(pl.multiple_of(zh * PAIR, PAIR), ROWS)
    CHUNK = 16

    def weights(ty, tx, acc):
        lse = cl[tx]
        for c in range(PAIR // CHUNK):
            at = pl.ds(pl.multiple_of(ty * PAIR + c * CHUNK, CHUNK), CHUNK)
            v = lg[tx, at]
            row = rl[at]
            g = jnp.exp2(v - jnp.concatenate([row] * 4, axis=1)) + jnp.exp2(v - lse)
            acc = acc + fold(g * v, jnp.sum)
            wt[tx, at] = (g * half_scale).astype(BF16)
        return acc

    acc = jnp.zeros((8, QUAD), F32)
    for t in reversed(range(STEPS)):

        def tile_weights(i, acc, t=t):
            row_part = i <= t
            tr = jnp.where(row_part, t, i - t - 1)
            tc = jnp.where(row_part, i, t)
            return weights(row_at(tr), col_at(tc), acc)

        if t < X and t < Y:
            acc = lax.fori_loop(0, 2 * t + 1, tile_weights, acc)
        elif t < X:
            acc = lax.fori_loop(
                0, Y, lambda i, a, t=t: weights(row_at(i), col_at(t), a), acc
            )
        else:
            acc = lax.fori_loop(
                0, X, lambda i, a, t=t: weights(row_at(t), col_at(i), a), acc
            )
        if t == 0:
            v = lg[x, own_at, own_cols]
            lse = cl[x, :, own_cols]
            g = jnp.exp2(v - rl[own_at]) + jnp.exp2(v - lse)
            wt[x, own_at, own_cols] = (
                jnp.where(eye, g - 2.0, g) * half_scale[:, :ROWS]
            ).astype(BF16)
            diagonal = jnp.sum(jnp.where(eye, v, 0.0), axis=0, keepdims=True)
            loss = 0.5 * (to_lanes(rl[own_at]) + lse) - diagonal
            total = functools.reduce(jnp.add, lanes_of(jnp.sum(acc, axis=0, keepdims=True)))
            rows8 = lax.broadcasted_iota(jnp.int32, (8, ROWS), 0)
            sc1_recv[own_b] = (
                jnp.where(rows8 == 0, loss, jnp.where(rows8 == 1, 0.5 * total - diagonal, 0.0))
                * LN2
            )
        if t < X:
            tx = col_at(t)
            part = dot(et_all[...], wt[tx])
            for f in range(2):
                sib_send[2 * tx + f] = part[:, (2 * f + 1) * ROWS : (2 * f + 2) * ROWS].astype(BF16)
                own_part[2 * tx + f] = part[:, 2 * f * ROWS : (2 * f + 1) * ROWS]
            for f in range(2):
                s_copy(2 * tx + f).start()
        if t < Y:
            ty = row_at(t)
            total = functools.reduce(
                jnp.add,
                [
                    dot(wt[j, rows_of(ty)], i_all[pl.ds(2 * j, 2)].reshape(QUAD, D))
                    for j in range(X)
                ],
            )
            de_send[pl.ds(2 * ty, 2)] = total.astype(BF16).reshape(2, ROWS, D)
            for k in (2 * t, 2 * t + 1):
                if k > 0:
                    de_copy(k, row_member(k)[1], own_b).start()
        if t < X:
            for k in (2 * t, 2 * t + 1):
                _, j = col_member(k, 0)
                s_copy(j).wait_recv()
                total = own_part[j] + sib_recv[j].astype(F32)
                if k > 0:
                    di_send[j] = total.astype(BF16)
                    di_copy(k, j, own_j).start()
                else:
                    di_recv[j] = total.astype(BF16)

    def a_copy(k, slot):
        device, _ = row_member(k)
        return remote(sc1_recv.at[slot], sc1_recv.at[slot], a_ss.at[k], a_rs.at[slot], device)

    for k in range(1, NB):
        a_copy(k, own_b).start()
    for k in range(1, NB):
        r_copy(k, own_b).wait_send()
    for r in range(2):
        for k in range(1 - r, NJ):
            c_copy(k, r, own_j * 2 + r).wait_send()
    for k in range(1, NB):
        _, b = row_member(k)
        a_copy(0, b).wait_recv()
    sc2_recv[own_j * 2] = jnp.sum(sc1_recv[...], axis=0)

    def b_copy(k, r, slot):
        device, _ = col_member(k, r)
        return remote(
            sc2_recv.at[own_j * 2], sc2_recv.at[slot], b_ss.at[r, k], b_rs.at[slot], device
        )

    for r in range(2):
        for k in range(1 - r, NJ):
            b_copy(k, r, own_j * 2 + r).start()

    for k in range(1, NB):
        a_copy(k, own_b).wait_send()
    for k in range(NJ):
        s_copy(col_member(k, 0)[1]).wait_send()
    for k in range(1, NJ):
        di_copy(k, col_member(k, 0)[1], own_j).wait_send()
    for k in range(1, NB):
        de_copy(k, row_member(k)[1], own_b).wait_send()
    for r in range(2):
        for k in range(1 - r, NJ):
            b_copy(k, r, own_j * 2 + r).wait_send()

    def finish(field_ref, inv, direction, place):
        unit = field_ref[...] * inv
        grads_ref[place] = inv * (
            direction - unit * jnp.sum(unit * direction, axis=1, keepdims=True)
        )

    for k in range(1, NJ):
        _, j = col_member(k, 0)
        di_copy(0, j, j).wait_recv()
    total = di_recv[0].astype(F32)
    for j in range(1, NJ):
        total = total + di_recv[j].astype(F32)
    finish(im_ref, inv_i, total.T, 1)

    de_recv[own_b] = de_send[own_b]
    for k in range(1, NB):
        _, b = row_member(k)
        de_copy(0, b, b).wait_recv()
    total = de_recv[0].astype(F32)
    for b in range(1, NB):
        total = total + de_recv[b].astype(F32)
    finish(ev_ref, inv_e, total, 0)

    for r in range(2):
        for k in range(1 - r, NJ):
            _, j = col_member(k, r)
            b_copy(0, r, j * 2 + r).wait_recv()
    sums_ref[...] = jnp.sum(sc2_recv[...], axis=0) * (1.0 / (NB * NJ * 2 * ROWS))


def write(grads_ref, sums_ref, eg_hbm, ig_hbm, loss_hbm, sg_hbm, loss_ref, sg_ref, sems):
    copies = [
        pltpu.make_async_copy(grads_ref.at[0], eg_hbm, sems.at[0]),
        pltpu.make_async_copy(grads_ref.at[1], ig_hbm, sems.at[1]),
        pltpu.make_async_copy(loss_ref, loss_hbm, sems.at[2]),
        pltpu.make_async_copy(sg_ref, sg_hbm, sems.at[3]),
    ]
    for copy in copies[:2]:
        copy.start()
    loss_ref[0] = jnp.sum(sums_ref[0:1])
    sg_ref[0] = jnp.sum(sums_ref[1:2])
    for copy in copies[2:]:
        copy.start()
    for copy in copies:
        copy.wait()


def solution(mesh):
    X, Y = mesh.shape["dx"] // 4, mesh.shape["dy"] // 2
    NB, NJ = 2 * Y, 2 * X

    def on_device(events, images, log_scale):
        rows, D = events.shape
        dma = pltpu.SemaphoreType.DMA
        vmem = pl.BlockSpec(memory_space=pltpu.VMEM)
        hbm = pl.BlockSpec(memory_space=pltpu.HBM)
        block = jax.ShapeDtypeStruct((rows, D), F32)
        scalar = jax.ShapeDtypeStruct((1,), F32)
        V = pltpu.VMEM
        grads, sums = pl.pallas_call(
            functools.partial(kernel, X, Y),
            out_shape=(
                jax.ShapeDtypeStruct((2, rows, D), F32),
                jax.ShapeDtypeStruct((8, ROWS), F32),
            ),
            in_specs=[hbm, hbm, hbm],
            out_specs=(vmem, vmem),
            scratch_shapes=[
                V((rows, D), F32),
                V((rows, D), F32),
                pltpu.SMEM((1,), F32),
                V((NB, ROWS, D), BF16),
                V((D, NB * ROWS), BF16),
                V((NJ, 2 * ROWS, D), BF16),
                V((X, D, 4 * ROWS), BF16),
                V((X, NB * ROWS, 4 * ROWS), F32),
                V((X, NB * ROWS, 4 * ROWS), BF16),
                V((NB * ROWS, ROWS), F32),
                V((NB * ROWS, ROWS), F32),
                V((X, 8, 4 * ROWS), F32),
                V((X, 8, 4 * ROWS), F32),
                V((NB * ROWS, ROWS), F32),
                V((X, 1, 4 * ROWS), F32),
                V((NB, NB, ROWS), F32),
                V((2 * NJ, ROWS), F32),
                V((2 * NJ, ROWS), F32),
                V((2 * NJ, 2 * NJ, ROWS), F32),
                V((NJ, D, ROWS), BF16),
                V((NJ, D, ROWS), BF16),
                V((NJ, D, ROWS), F32),
                V((NJ, D, ROWS), BF16),
                V((NJ, D, ROWS), BF16),
                V((NB, ROWS, D), BF16),
                V((NB, ROWS, D), BF16),
                V((NB, 8, ROWS), F32),
                V((2 * NJ, 8, ROWS), F32),
                dma((3,)),
                dma((NB,)),
                dma((NB,)),
                dma((NJ,)),
                dma((NJ,)),
                dma((NJ,)),
                dma((NJ,)),
                dma((NB,)),
                dma((NB,)),
                dma((2, NJ)),
                dma((2 * NJ,)),
                dma((NJ,)),
                dma((NJ,)),
                dma((NJ,)),
                dma((NJ,)),
                dma((NB,)),
                dma((NB,)),
                dma((NB,)),
                dma((NB,)),
                dma((2, NJ)),
                dma((2 * NJ,)),
            ],
            compiler_params=pltpu.CompilerParams(
                collective_id=0,
                has_side_effects=True,
                vmem_limit_bytes=60 * 1024 * 1024,
            ),
        )(events, images, log_scale)
        return pl.pallas_call(
            write,
            out_shape=(block, block, scalar, scalar),
            in_specs=[vmem, vmem],
            out_specs=(hbm, hbm, hbm, hbm),
            scratch_shapes=[pltpu.SMEM((1,), F32), pltpu.SMEM((1,), F32), dma((4,))],
        )(grads, sums)

    return jax.shard_map(
        on_device,
        mesh=mesh,
        in_specs=(P(("dx", "dy"), None), P(("dx", "dy"), None), P()),
        out_specs=(P(("dx", "dy"), None), P(("dx", "dy"), None), P(), P()),
        check_vma=False,
    )
```

```python
import functools

import jax
import jax.numpy as jnp
from jax import lax
from jax.experimental import pallas as pl
from jax.experimental.pallas import tpu as pltpu
from jax.sharding import PartitionSpec as P

EPSILON = 1e-06
MESH = pl.DeviceIdType.MESH
LOG2E = 1.4426950408889634
LN2 = 0.6931471805599453
ROWS = 128
F32 = jnp.float32
BF16 = jnp.bfloat16


def members(n):
    ring = [s for s in (1, n - 1, 2) if 0 < s < n]
    ring = list(dict.fromkeys(ring))
    places = [(0, 0), (0, 1)] + [(s, 0) for s in ring] + [(s, 1) for s in ring]
    back = [places.index((-s % n, f)) for s, f in places]
    return places, back


def dot(a, b):
    return lax.dot_general(a, b, (((1,), (0,)), ((), ())), preferred_element_type=F32)


def kernel(
    X,
    Y,
    ev_hbm,
    im_hbm,
    ls_hbm,
    grads_ref,
    sums_ref,
    ev_ref,
    im_ref,
    ls_ref,
    e_all,
    et_all,
    i_all,
    it_all,
    lg,
    wt,
    rm,
    rs,
    ru,
    cm,
    cs,
    cu,
    rl,
    cl,
    lanes_ref,
    row_recv,
    col_b,
    col_recv,
    sib_send,
    sib_recv,
    own_part,
    di_send,
    di_recv,
    de_send,
    de_recv,
    sc1_recv,
    sc2_recv,
    in_s,
    e_ss,
    e_rs,
    i_ss,
    i_rs,
    f_ss,
    f_rs,
    r_ss,
    r_rs,
    c_ss,
    c_rs,
    s_ss,
    s_rs,
    di_ss,
    di_rs,
    de_ss,
    de_rs,
    a_ss,
    a_rs,
    b_ss,
    b_rs,
):
    NB, NJ = 2 * Y, 2 * X
    STEPS = max(X, Y)
    D = ev_ref.shape[1]
    PAIR, QUAD, HALF = 2 * ROWS, 4 * ROWS, ROWS // 2
    dx, dy = lax.axis_index("dx"), lax.axis_index("dy")
    core, zl, x = dx % 2, (dx // 2) % 2, dx // 4
    y, zh = dy % Y, dy // Y
    row_places, row_back = members(Y)
    col_places, col_back = members(X)

    def row_device(k):
        s, f = row_places[k]
        return ((x * 2 + (zl ^ f)) * 2 + core, zh * Y + (y + s) % Y)

    def row_number(k):
        s, f = row_places[k]
        return (y + s) % Y * 2 + (zl ^ f)

    def col_device(k, r=0):
        s, f = col_places[k]
        return (((x + s) % X * 2 + (zl ^ f)) * 2 + (core ^ r), (zh ^ f) * Y + y)

    def col_number(k):
        s, f = col_places[k]
        return (x + s) % X * 2 + (zh ^ f)

    def remote(src, dst, ss, rsem, device):
        return pltpu.make_async_remote_copy(
            src_ref=src,
            dst_ref=dst,
            send_sem=ss,
            recv_sem=rsem,
            device_id=device,
            device_id_type=MESH,
        )

    loads = [
        pltpu.make_async_copy(ev_hbm, ev_ref, in_s.at[0]),
        pltpu.make_async_copy(im_hbm, im_ref, in_s.at[1]),
        pltpu.make_async_copy(ls_hbm, ls_ref, in_s.at[2]),
    ]
    for load in loads:
        load.start()
    barrier = pltpu.get_barrier_semaphore()
    for k in range(1, NB):
        pl.semaphore_signal(barrier, inc=1, device_id=row_device(k), device_id_type=MESH)
    for r in range(2):
        for k in range(1 - r, NJ):
            pl.semaphore_signal(barrier, inc=1, device_id=col_device(k, r), device_id_type=MESH)
    for load in loads:
        load.wait()

    def inverse(ref):
        v = ref[...]
        return lax.rsqrt(jnp.sum(v * v, axis=1, keepdims=True) + EPSILON)

    inv_e, inv_i = inverse(ev_ref), inverse(im_ref)
    e_all[0] = (ev_ref[...] * inv_e).astype(BF16)
    i_all[0, 0:ROWS] = (im_ref[...] * inv_i).astype(BF16)
    scale = jnp.exp(jnp.full((1, ROWS), ls_ref[0], F32))
    scale4 = jnp.concatenate([scale] * 4, axis=1)
    to_base2 = scale4 * LOG2E
    for ref in (rm, cm):
        ref[...] = jnp.full(ref.shape, -1e30, F32)
    for ref in (rs, ru, cs, cu):
        ref[...] = jnp.zeros(ref.shape, F32)

    pl.semaphore_wait(barrier, (NB - 1) + (2 * NJ - 1))

    sent = []

    def block(ref, k, half):
        rows = pl.ds(0, ROWS) if half is None else pl.ds(half * HALF, HALF)
        return ref.at[k, rows]

    def e_copy(n, src, dst, half, k):
        sem = e_rs.at[dst, half or 0]
        return remote(block(e_all, src, half), block(e_all, dst, half), e_ss.at[n], sem, row_device(k))

    def i_copy(n, src, dst, half, k):
        sem = i_rs.at[dst, half or 0]
        return remote(block(i_all, src, half), block(i_all, dst, half), i_ss.at[n], sem, col_device(k))

    def f_copy(k):
        half = i_all.at[k, pl.ds(0, ROWS)]
        other = i_all.at[k, pl.ds(ROWS, ROWS)]
        return remote(half, other, f_ss.at[k], f_rs.at[k], col_device(0, 1))

    def send(copy):
        copy.start()
        sent.append(copy)

    def first_sends(k):
        for make, places, back in ((e_copy, row_places, row_back), (i_copy, col_places, col_back)):
            if k < len(places) and places[k][0] * places[k][1] == 0:
                send(make(k, 0, back[k], None, k))

    def take(make, places, back, k):
        count = len(places)
        step, far = places[k]
        if step and far:
            for half in range(2):
                make(0, 0, k, half, k).wait_recv()
        elif k > 0:
            make(0, 0, k, None, k).wait_recv()
        if far and not step:
            for m in range(2, count):
                if places[m][1] == 0:
                    to = places.index((-places[m][0] % (count // 2), 1))
                    send(make(count + m, 1, to, 0, m))
        elif step and not far:
            send(make(2 * count + k, k, places.index((step, 1)), 1, 1))

    send(f_copy(0))
    for k in range(1, max(NB, NJ)):
        first_sends(k)

    eye = lax.broadcasted_iota(jnp.int32, (ROWS, ROWS), 0) == lax.broadcasted_iota(
        jnp.int32, (ROWS, ROWS), 1
    )

    def to_lanes(column):
        return jnp.sum(jnp.where(eye, column, 0.0), axis=0, keepdims=True)

    def to_rows(lanes):
        return jnp.sum(jnp.where(eye, lanes, 0.0), axis=1, keepdims=True)

    def lanes_of(v):
        return [v[:, ROWS * c : ROWS * (c + 1)] for c in range(v.shape[1] // ROWS)]

    def fold(v, op):
        return op(v.reshape(v.shape[0] // 8, 8, v.shape[1]), axis=0)

    def total_of(terms):
        return functools.reduce(jnp.add, terms)

    def tile(tr, tc):
        at = pl.ds(tr * PAIR, PAIR)
        v = dot(e_all[2 * tr : 2 * tr + 2].reshape(PAIR, D), it_all[tc]) * to_base2
        lg[tc, at] = v
        parts = lanes_of(v)
        old = rm[at]
        new = functools.reduce(jnp.maximum, parts, old)
        terms = [jnp.exp2(p - new) for p in parts]
        keep = jnp.exp2(old - new)
        rs[at] = rs[at] * keep + total_of(terms)
        ru[at] = ru[at] * keep + total_of([e * p for e, p in zip(terms, parts)])
        rm[at] = new
        old = cm[tc]
        new = jnp.maximum(old, fold(v, jnp.max))
        v = v.reshape(PAIR // 8, 8, QUAD)
        terms = jnp.exp2(v - new[None])
        keep = jnp.exp2(old - new)
        cs[tc] = cs[tc] * keep + jnp.sum(terms, axis=0)
        cu[tc] = cu[tc] * keep + jnp.sum(terms * v, axis=0)
        cm[tc] = new

    for t in range(STEPS):
        for k in (2 * t, 2 * t + 1):
            if t < X:
                take(i_copy, col_places, col_back, k)
                if k > 0:
                    send(f_copy(k))
            if t < Y:
                take(e_copy, row_places, row_back, k)
        if t < Y:
            et_all[:, t * PAIR : (t + 1) * PAIR] = e_all[2 * t : 2 * t + 2].reshape(PAIR, D).T
            for u in range(min(t, X)):
                tile(t, u)
        if t < X:
            for k in (2 * t, 2 * t + 1):
                f_copy(k).wait_recv()
            it_all[t] = i_all[2 * t : 2 * t + 2].reshape(QUAD, D).T
            for u in range(min(t + 1, Y)):
                tile(u, t)

    def r_copy(k, slot):
        return remote(row_recv.at[0], row_recv.at[slot], r_ss.at[k], r_rs.at[slot], row_device(k))

    def c_copy(k, r, slot):
        src = col_b if r else col_recv.at[0]
        return remote(src, col_recv.at[slot], c_ss.at[r, k], c_rs.at[slot], col_device(k, r))

    for b in range(NB):
        at = pl.ds(b * ROWS, ROWS)
        v = rm[at]
        top = jnp.max(v, axis=1, keepdims=True)
        share = jnp.exp2(v - top)
        tot = jnp.sum(rs[at] * share, axis=1, keepdims=True)
        mean = jnp.sum(ru[at] * share, axis=1, keepdims=True) / tot
        number = row_number(b)
        row_recv[0, pl.ds(number, 1)] = to_lanes(top + jnp.log2(tot))
        row_recv[0, pl.ds(NB + number, 1)] = to_lanes(mean)
    for k in range(1, NB):
        r_copy(k, row_back[k]).start()
    for t in range(X):
        v = cm[t]
        top = jnp.max(v, axis=0, keepdims=True)
        share = jnp.exp2(v - top)
        tot = jnp.sum(cs[t] * share, axis=0, keepdims=True)
        mean = jnp.sum(cu[t] * share, axis=0, keepdims=True) / tot
        lse = lanes_of(top + jnp.log2(tot))
        mean = lanes_of(mean)
        for c in range(4):
            number = 2 * col_number(2 * t + c // 2)
            col_recv[0, pl.ds(number + c % 2, 1)] = lse[c]
            col_recv[0, pl.ds(2 * NJ + number + c % 2, 1)] = mean[c]
            col_b[pl.ds(number + 1 - c % 2, 1)] = lse[c]
            col_b[pl.ds(2 * NJ + number + 1 - c % 2, 1)] = mean[c]
    for r in range(2):
        for k in range(1 - r, NJ):
            c_copy(k, r, col_back[k] + r * NJ).start()
    for copy in sent:
        copy.wait_send()
    for r in range(2):
        for k in range(1 - r, NJ):
            c_copy(0, r, k + r * NJ).wait_recv()

    def merge(lse, mean):
        top = jnp.max(lse, axis=0)
        share = jnp.exp2(lse - top[None])
        tot = jnp.sum(share, axis=0)
        return top + jnp.log2(tot), jnp.sum(share * mean, axis=0) / tot

    col_lse, col_mean = merge(col_recv[:, 0 : 2 * NJ], col_recv[:, 2 * NJ :])
    lanes_ref[0, 0 : 2 * NJ] = col_lse
    lanes_ref[1, 0 : 2 * NJ] = col_mean
    own_col = pl.ds(2 * col_number(0), 1)
    own_col_lse, own_col_mean = lanes_ref[0, own_col], lanes_ref[1, own_col]
    for t in range(X):
        cl[t] = jnp.concatenate(
            [
                lanes_ref[0, pl.ds(2 * col_number(2 * t + c // 2) + c % 2, 1)]
                for c in range(4)
            ],
            axis=1,
        )
    for k in range(1, NB):
        r_copy(0, k).wait_recv()
    row_lse, row_mean = merge(row_recv[:, 0:NB], row_recv[:, NB:])
    lanes_ref[2, 0:NB] = row_lse
    lanes_ref[3, 0:NB] = row_mean
    own_row = pl.ds(row_number(0), 1)
    own_row_lse, own_row_mean = lanes_ref[2, own_row], lanes_ref[3, own_row]
    for b in range(NB):
        row = lanes_ref[2, pl.ds(row_number(b), 1)]
        rl[pl.ds(b * ROWS, ROWS)] = jnp.broadcast_to(to_rows(row), (ROWS, ROWS))

    diagonal = jnp.sum(
        jnp.where(eye, lg[0, 0:ROWS, 0:ROWS], 0.0), axis=0, keepdims=True
    )
    loss = 0.5 * (own_row_lse + own_col_lse) - diagonal
    slope = 0.5 * (own_row_mean + own_col_mean) - diagonal
    rows8 = lax.broadcasted_iota(jnp.int32, (8, ROWS), 0)
    sc1_recv[0] = jnp.where(rows8 == 0, loss, jnp.where(rows8 == 1, slope, 0.0)) * LN2

    def a_copy(k, slot):
        return remote(sc1_recv.at[0], sc1_recv.at[slot], a_ss.at[k], a_rs.at[slot], row_device(k))

    for k in range(1, NB):
        a_copy(k, row_back[k]).start()

    half_scale = 0.5 * scale4
    CHUNK = 16

    def s_copy(k):
        return remote(
            sib_send.at[k], sib_recv.at[k], s_ss.at[k], s_rs.at[k], col_device(0, 1)
        )

    def di_copy(k, slot):
        return remote(di_send.at[k], di_recv.at[slot], di_ss.at[k], di_rs.at[slot], col_device(k))

    def de_copy(k, slot):
        return remote(de_send.at[k], de_recv.at[slot], de_ss.at[k], de_rs.at[slot], row_device(k))

    def weights(tr, tc):
        lse = cl[tc]
        for c in range(PAIR // CHUNK):
            at = pl.ds(pl.multiple_of(tr * PAIR + c * CHUNK, CHUNK), CHUNK)
            v = lg[tc, at]
            row = rl[at]
            g = jnp.exp2(v - jnp.concatenate([row] * 4, axis=1)) + jnp.exp2(v - lse)
            wt[tc, at] = (g * half_scale).astype(BF16)
        return 0

    def pass_on(t):
        for k in (2 * t, 2 * t + 1):
            s_copy(k).wait_recv()
            total = (own_part[k] + sib_recv[k].astype(F32)).astype(BF16)
            if k > 0:
                di_send[k] = total
                di_copy(k, col_back[k]).start()
            else:
                di_recv[0] = total

    for t in reversed(range(STEPS)):
        if t < Y:
            lax.fori_loop(0, min(t + 1, X), lambda i, _, t=t: weights(t, i), 0)
        if t == 0:
            v = lg[0, 0:ROWS, 0:ROWS]
            g = jnp.exp2(v - rl[0:ROWS]) + jnp.exp2(v - cl[0, :, 0:ROWS])
            wt[0, 0:ROWS, 0:ROWS] = (
                jnp.where(eye, g - 2.0, g) * half_scale[:, :ROWS]
            ).astype(BF16)
        if t < Y:
            at = slice(t * PAIR, (t + 1) * PAIR)
            total = total_of(
                [
                    dot(wt[j, at], i_all[2 * j : 2 * j + 2].reshape(QUAD, D))
                    for j in range(X)
                ]
            )
            total = total.astype(BF16).reshape(2, ROWS, D)
            for f in range(2):
                k = 2 * t + f
                if k > 0:
                    de_send[k] = total[f]
                    de_copy(k, row_back[k]).start()
                else:
                    de_recv[0] = total[f]
        if t + 1 < X:
            pass_on(t + 1)
        if t < X:
            if t > 0:
                lax.fori_loop(0, min(t, Y), lambda i, _, t=t: weights(i, t), 0)
            part = dot(et_all[...], wt[t])
            for f in range(2):
                sib_send[2 * t + f] = part[:, (2 * f + 1) * ROWS : (2 * f + 2) * ROWS].astype(BF16)
                own_part[2 * t + f] = part[:, 2 * f * ROWS : (2 * f + 1) * ROWS]
            for f in range(2):
                s_copy(2 * t + f).start()
    pass_on(0)

    for k in range(1, NB):
        a_copy(0, k).wait_recv()
    sc2_recv[0] = jnp.sum(sc1_recv[...], axis=0)

    def b_copy(k, r, slot):
        return remote(
            sc2_recv.at[0], sc2_recv.at[slot], b_ss.at[r, k], b_rs.at[slot], col_device(k, r)
        )

    for r in range(2):
        for k in range(1 - r, NJ):
            b_copy(k, r, col_back[k] + r * NJ).start()
    for k in range(1, NB):
        r_copy(k, row_back[k]).wait_send()
        a_copy(k, row_back[k]).wait_send()
        de_copy(k, row_back[k]).wait_send()
    for k in range(NJ):
        s_copy(k).wait_send()
        if k > 0:
            di_copy(k, col_back[k]).wait_send()
    for r in range(2):
        for k in range(1 - r, NJ):
            c_copy(k, r, col_back[k] + r * NJ).wait_send()
            b_copy(k, r, col_back[k] + r * NJ).wait_send()

    def finish(field_ref, inv, direction, place):
        unit = field_ref[...] * inv
        grads_ref[place] = inv * (
            direction - unit * jnp.sum(unit * direction, axis=1, keepdims=True)
        )

    for k in range(1, NJ):
        di_copy(0, k).wait_recv()
    finish(im_ref, inv_i, total_of([di_recv[k].astype(F32) for k in range(NJ)]).T, 1)
    for k in range(1, NB):
        de_copy(0, k).wait_recv()
    finish(ev_ref, inv_e, total_of([de_recv[k].astype(F32) for k in range(NB)]), 0)
    for r in range(2):
        for k in range(1 - r, NJ):
            b_copy(0, r, k + r * NJ).wait_recv()
    sums_ref[...] = jnp.sum(sc2_recv[...], axis=0) * (1.0 / (NB * NJ * 2 * ROWS))


def write(grads_ref, sums_ref, eg_hbm, ig_hbm, loss_hbm, sg_hbm, loss_ref, sg_ref, sems):
    copies = [
        pltpu.make_async_copy(grads_ref.at[0], eg_hbm, sems.at[0]),
        pltpu.make_async_copy(grads_ref.at[1], ig_hbm, sems.at[1]),
        pltpu.make_async_copy(loss_ref, loss_hbm, sems.at[2]),
        pltpu.make_async_copy(sg_ref, sg_hbm, sems.at[3]),
    ]
    for copy in copies[:2]:
        copy.start()
    loss_ref[0] = jnp.sum(sums_ref[0:1])
    sg_ref[0] = jnp.sum(sums_ref[1:2])
    for copy in copies[2:]:
        copy.start()
    for copy in copies:
        copy.wait()


def solution(mesh):
    X, Y = mesh.shape["dx"] // 4, mesh.shape["dy"] // 2
    NB, NJ = 2 * Y, 2 * X

    def on_device(events, images, log_scale):
        rows, D = events.shape
        dma = pltpu.SemaphoreType.DMA
        vmem = pl.BlockSpec(memory_space=pltpu.VMEM)
        hbm = pl.BlockSpec(memory_space=pltpu.HBM)
        block = jax.ShapeDtypeStruct((rows, D), F32)
        scalar = jax.ShapeDtypeStruct((1,), F32)
        V = pltpu.VMEM
        grads, sums = pl.pallas_call(
            functools.partial(kernel, X, Y),
            out_shape=(
                jax.ShapeDtypeStruct((2, rows, D), F32),
                jax.ShapeDtypeStruct((8, ROWS), F32),
            ),
            in_specs=[hbm, hbm, hbm],
            out_specs=(vmem, vmem),
            scratch_shapes=[
                V((rows, D), F32),
                V((rows, D), F32),
                pltpu.SMEM((1,), F32),
                V((NB, ROWS, D), BF16),
                V((D, NB * ROWS), BF16),
                V((NJ, 2 * ROWS, D), BF16),
                V((X, D, 4 * ROWS), BF16),
                V((X, NB * ROWS, 4 * ROWS), F32),
                V((X, NB * ROWS, 4 * ROWS), BF16),
                V((NB * ROWS, ROWS), F32),
                V((NB * ROWS, ROWS), F32),
                V((NB * ROWS, ROWS), F32),
                V((X, 8, 4 * ROWS), F32),
                V((X, 8, 4 * ROWS), F32),
                V((X, 8, 4 * ROWS), F32),
                V((NB * ROWS, ROWS), F32),
                V((X, 1, 4 * ROWS), F32),
                V((4, max(NB, 2 * NJ), ROWS), F32),
                V((NB, 2 * NB, ROWS), F32),
                V((4 * NJ, ROWS), F32),
                V((2 * NJ, 4 * NJ, ROWS), F32),
                V((NJ, D, ROWS), BF16),
                V((NJ, D, ROWS), BF16),
                V((NJ, D, ROWS), F32),
                V((NJ, D, ROWS), BF16),
                V((NJ, D, ROWS), BF16),
                V((NB, ROWS, D), BF16),
                V((NB, ROWS, D), BF16),
                V((NB, 8, ROWS), F32),
                V((2 * NJ, 8, ROWS), F32),
                dma((3,)),
                dma((3 * NB,)),
                dma((NB, 2)),
                dma((3 * NJ,)),
                dma((NJ, 2)),
                dma((NJ,)),
                dma((NJ,)),
                dma((NB,)),
                dma((NB,)),
                dma((2, NJ)),
                dma((2 * NJ,)),
                dma((NJ,)),
                dma((NJ,)),
                dma((NJ,)),
                dma((NJ,)),
                dma((NB,)),
                dma((NB,)),
                dma((NB,)),
                dma((NB,)),
                dma((2, NJ)),
                dma((2 * NJ,)),
            ],
            compiler_params=pltpu.CompilerParams(
                collective_id=0,
                has_side_effects=True,
                vmem_limit_bytes=60 * 1024 * 1024,
            ),
        )(events, images, log_scale)
        return pl.pallas_call(
            write,
            out_shape=(block, block, scalar, scalar),
            in_specs=[vmem, vmem],
            out_specs=(hbm, hbm, hbm, hbm),
            scratch_shapes=[pltpu.SMEM((1,), F32), pltpu.SMEM((1,), F32), dma((4,))],
        )(grads, sums)

    return jax.shard_map(
        on_device,
        mesh=mesh,
        in_specs=(P(("dx", "dy"), None), P(("dx", "dy"), None), P()),
        out_specs=(P(("dx", "dy"), None), P(("dx", "dy"), None), P(), P()),
        check_vma=False,
    )
```

```python
import functools

import jax
import jax.numpy as jnp
from jax import lax
from jax.experimental import pallas as pl
from jax.experimental.pallas import tpu as pltpu
from jax.sharding import PartitionSpec as P

EPSILON = 1e-06
MESH = pl.DeviceIdType.MESH
LOG2E = 1.4426950408889634
LN2 = 0.6931471805599453
ROWS = 128
F32 = jnp.float32
BF16 = jnp.bfloat16


def members(n):
    ring = [s for s in (1, n - 1, 2) if 0 < s < n]
    ring = list(dict.fromkeys(ring))
    places = [(0, 0), (0, 1)] + [(s, 0) for s in ring] + [(s, 1) for s in ring]
    back = [places.index((-s % n, f)) for s, f in places]
    return places, back


def dot(a, b):
    return lax.dot_general(a, b, (((1,), (0,)), ((), ())), preferred_element_type=F32)


def kernel(
    X,
    Y,
    ev_hbm,
    im_hbm,
    ls_hbm,
    grads_ref,
    sums_ref,
    ev_ref,
    im_ref,
    ls_ref,
    e_all,
    et_all,
    i_all,
    it_all,
    lg,
    wt,
    rm,
    rs,
    ru,
    cm,
    cs,
    cu,
    rl,
    cl,
    lanes_ref,
    row_recv,
    col_b,
    col_recv,
    sib_send,
    sib_recv,
    own_part,
    di_send,
    di_mid,
    di_recv,
    de_part,
    de_send,
    de_mid,
    de_recv,
    sc1_recv,
    sc2_recv,
    sc3_recv,
    in_s,
    e_ss,
    e_rs,
    i_ss,
    i_rs,
    f_ss,
    f_rs,
    r_ss,
    r_rs,
    c_ss,
    c_rs,
    s_ss,
    s_rs,
    di_ss,
    di_ms,
    di_rs,
    de_ss,
    de_ms,
    de_rs,
    a_ss,
    a_rs,
    b_ss,
    b_rs,
    o_ss,
    o_rs,
):
    NB, NJ = 2 * Y, 2 * X
    STEPS = max(X, Y)
    D = ev_ref.shape[1]
    PAIR, QUAD, HALF = 2 * ROWS, 4 * ROWS, ROWS // 2
    dx, dy = lax.axis_index("dx"), lax.axis_index("dy")
    core, zl, x = dx % 2, (dx // 2) % 2, dx // 4
    y, zh = dy % Y, dy // Y
    row_places, row_back = members(Y)
    col_places, col_back = members(X)

    def row_device(k):
        s, f = row_places[k]
        return ((x * 2 + (zl ^ f)) * 2 + core, zh * Y + (y + s) % Y)

    def row_number(k):
        s, f = row_places[k]
        return (y + s) % Y * 2 + (zl ^ f)

    def col_device(k, r=0):
        s, f = col_places[k]
        return (((x + s) % X * 2 + (zl ^ f)) * 2 + (core ^ r), (zh ^ f) * Y + y)

    def col_number(k):
        s, f = col_places[k]
        return (x + s) % X * 2 + (zh ^ f)

    def remote(src, dst, ss, rsem, device):
        return pltpu.make_async_remote_copy(
            src_ref=src,
            dst_ref=dst,
            send_sem=ss,
            recv_sem=rsem,
            device_id=device,
            device_id_type=MESH,
        )

    loads = [
        pltpu.make_async_copy(ev_hbm, ev_ref, in_s.at[0]),
        pltpu.make_async_copy(im_hbm, im_ref, in_s.at[1]),
        pltpu.make_async_copy(ls_hbm, ls_ref, in_s.at[2]),
    ]
    for load in loads:
        load.start()
    barrier = pltpu.get_barrier_semaphore()
    for k in range(1, NB):
        pl.semaphore_signal(barrier, inc=1, device_id=row_device(k), device_id_type=MESH)
    for r in range(2):
        for k in range(1 - r, NJ):
            pl.semaphore_signal(barrier, inc=1, device_id=col_device(k, r), device_id_type=MESH)
    for load in loads:
        load.wait()

    def inverse(ref):
        v = ref[...]
        return lax.rsqrt(jnp.sum(v * v, axis=1, keepdims=True) + EPSILON)

    inv_e, inv_i = inverse(ev_ref), inverse(im_ref)
    e_all[0] = (ev_ref[...] * inv_e).astype(BF16)
    i_all[0, 0:ROWS] = (im_ref[...] * inv_i).astype(BF16)
    scale = jnp.exp(jnp.full((1, ROWS), ls_ref[0], F32))
    scale4 = jnp.concatenate([scale] * 4, axis=1)
    to_base2 = scale4 * LOG2E
    for ref in (rm, cm):
        ref[...] = jnp.full(ref.shape, -1e30, F32)
    for ref in (rs, ru, cs, cu):
        ref[...] = jnp.zeros(ref.shape, F32)

    pl.semaphore_wait(barrier, (NB - 1) + (2 * NJ - 1))

    sent = []

    def block(ref, k, half):
        rows = pl.ds(0, ROWS) if half is None else pl.ds(half * HALF, HALF)
        return ref.at[k, rows]

    def e_copy(n, src, dst, half, k):
        sem = e_rs.at[dst, half or 0]
        return remote(block(e_all, src, half), block(e_all, dst, half), e_ss.at[n], sem, row_device(k))

    def i_copy(n, src, dst, half, k):
        sem = i_rs.at[dst, half or 0]
        return remote(block(i_all, src, half), block(i_all, dst, half), i_ss.at[n], sem, col_device(k))

    def f_copy(k):
        half = i_all.at[k, pl.ds(0, ROWS)]
        other = i_all.at[k, pl.ds(ROWS, ROWS)]
        return remote(half, other, f_ss.at[k], f_rs.at[k], col_device(0, 1))

    def send(copy):
        copy.start()
        sent.append(copy)

    def first_sends(k):
        for make, places, back in ((e_copy, row_places, row_back), (i_copy, col_places, col_back)):
            if k < len(places) and places[k][0] * places[k][1] == 0:
                send(make(k, 0, back[k], None, k))

    def take(make, places, back, k):
        count = len(places)
        step, far = places[k]
        if step and far:
            for half in range(2):
                make(0, 0, k, half, k).wait_recv()
        elif k > 0:
            make(0, 0, k, None, k).wait_recv()
        if far and not step:
            for m in range(2, count):
                if places[m][1] == 0:
                    to = places.index((-places[m][0] % (count // 2), 1))
                    send(make(count + m, 1, to, 0, m))
        elif step and not far:
            send(make(2 * count + k, k, places.index((step, 1)), 1, 1))

    send(f_copy(0))
    for k in range(1, max(NB, NJ)):
        first_sends(k)

    eye = lax.broadcasted_iota(jnp.int32, (ROWS, ROWS), 0) == lax.broadcasted_iota(
        jnp.int32, (ROWS, ROWS), 1
    )

    def to_lanes(column):
        return jnp.sum(jnp.where(eye, column, 0.0), axis=0, keepdims=True)

    def to_rows(lanes):
        return jnp.sum(jnp.where(eye, lanes, 0.0), axis=1, keepdims=True)

    def lanes_of(v):
        return [v[:, ROWS * c : ROWS * (c + 1)] for c in range(v.shape[1] // ROWS)]

    def fold(v, op):
        return op(v.reshape(v.shape[0] // 8, 8, v.shape[1]), axis=0)

    def total_of(terms):
        return functools.reduce(jnp.add, terms)

    def tile(tr, tc):
        at = pl.ds(tr * PAIR, PAIR)
        v = dot(e_all[2 * tr : 2 * tr + 2].reshape(PAIR, D), it_all[tc]) * to_base2
        lg[tc, at] = v
        parts = lanes_of(v)
        old = rm[at]
        new = functools.reduce(jnp.maximum, parts, old)
        terms = [jnp.exp2(p - new) for p in parts]
        keep = jnp.exp2(old - new)
        rs[at] = rs[at] * keep + total_of(terms)
        ru[at] = ru[at] * keep + total_of([e * p for e, p in zip(terms, parts)])
        rm[at] = new
        old = cm[tc]
        new = jnp.maximum(old, fold(v, jnp.max))
        v = v.reshape(PAIR // 8, 8, QUAD)
        terms = jnp.exp2(v - new[None])
        keep = jnp.exp2(old - new)
        cs[tc] = cs[tc] * keep + jnp.sum(terms, axis=0)
        cu[tc] = cu[tc] * keep + jnp.sum(terms * v, axis=0)
        cm[tc] = new

    for t in range(STEPS):
        for k in (2 * t, 2 * t + 1):
            if t < X:
                take(i_copy, col_places, col_back, k)
                if k > 0:
                    send(f_copy(k))
            if t < Y:
                take(e_copy, row_places, row_back, k)
        if t < Y:
            et_all[:, t * PAIR : (t + 1) * PAIR] = e_all[2 * t : 2 * t + 2].reshape(PAIR, D).T
            for u in range(min(t, X)):
                tile(t, u)
        if t < X:
            for k in (2 * t, 2 * t + 1):
                f_copy(k).wait_recv()
            it_all[t] = i_all[2 * t : 2 * t + 2].reshape(QUAD, D).T
            for u in range(min(t + 1, Y)):
                tile(u, t)

    def r_copy(k, slot):
        return remote(row_recv.at[0], row_recv.at[slot], r_ss.at[k], r_rs.at[slot], row_device(k))

    def c_copy(k, r, slot):
        src = col_b if r else col_recv.at[0]
        return remote(src, col_recv.at[slot], c_ss.at[r, k], c_rs.at[slot], col_device(k, r))

    for b in range(NB):
        at = pl.ds(b * ROWS, ROWS)
        v = rm[at]
        top = jnp.max(v, axis=1, keepdims=True)
        share = jnp.exp2(v - top)
        tot = jnp.sum(rs[at] * share, axis=1, keepdims=True)
        mean = jnp.sum(ru[at] * share, axis=1, keepdims=True) / tot
        number = row_number(b)
        row_recv[0, pl.ds(number, 1)] = to_lanes(top + jnp.log2(tot))
        row_recv[0, pl.ds(NB + number, 1)] = to_lanes(mean)
    for k in range(1, NB):
        r_copy(k, row_back[k]).start()
    for t in range(X):
        v = cm[t]
        top = jnp.max(v, axis=0, keepdims=True)
        share = jnp.exp2(v - top)
        tot = jnp.sum(cs[t] * share, axis=0, keepdims=True)
        mean = jnp.sum(cu[t] * share, axis=0, keepdims=True) / tot
        lse = lanes_of(top + jnp.log2(tot))
        mean = lanes_of(mean)
        for c in range(4):
            number = 2 * col_number(2 * t + c // 2)
            col_recv[0, pl.ds(number + c % 2, 1)] = lse[c]
            col_recv[0, pl.ds(2 * NJ + number + c % 2, 1)] = mean[c]
            col_b[pl.ds(number + 1 - c % 2, 1)] = lse[c]
            col_b[pl.ds(2 * NJ + number + 1 - c % 2, 1)] = mean[c]
    for r in range(2):
        for k in range(1 - r, NJ):
            c_copy(k, r, col_back[k] + r * NJ).start()
    for copy in sent:
        copy.wait_send()
    for r in range(2):
        for k in range(1 - r, NJ):
            c_copy(0, r, k + r * NJ).wait_recv()

    def merge(lse, mean):
        top = jnp.max(lse, axis=0)
        share = jnp.exp2(lse - top[None])
        tot = jnp.sum(share, axis=0)
        return top + jnp.log2(tot), jnp.sum(share * mean, axis=0) / tot

    col_lse, col_mean = merge(col_recv[:, 0 : 2 * NJ], col_recv[:, 2 * NJ :])
    lanes_ref[0, 0 : 2 * NJ] = col_lse
    lanes_ref[1, 0 : 2 * NJ] = col_mean
    own_col = pl.ds(2 * col_number(0), 1)
    own_col_lse, own_col_mean = lanes_ref[0, own_col], lanes_ref[1, own_col]
    for t in range(X):
        cl[t] = jnp.concatenate(
            [
                lanes_ref[0, pl.ds(2 * col_number(2 * t + c // 2) + c % 2, 1)]
                for c in range(4)
            ],
            axis=1,
        )
    for k in range(1, NB):
        r_copy(0, k).wait_recv()
    row_lse, row_mean = merge(row_recv[:, 0:NB], row_recv[:, NB:])
    lanes_ref[2, 0:NB] = row_lse
    lanes_ref[3, 0:NB] = row_mean
    own_row = pl.ds(row_number(0), 1)
    own_row_lse, own_row_mean = lanes_ref[2, own_row], lanes_ref[3, own_row]
    for b in range(NB):
        row = lanes_ref[2, pl.ds(row_number(b), 1)]
        rl[pl.ds(b * ROWS, ROWS)] = jnp.broadcast_to(to_rows(row), (ROWS, ROWS))

    diagonal = jnp.sum(
        jnp.where(eye, lg[0, 0:ROWS, 0:ROWS], 0.0), axis=0, keepdims=True
    )
    loss = 0.5 * (own_row_lse + own_col_lse) - diagonal
    slope = 0.5 * (own_row_mean + own_col_mean) - diagonal
    rows8 = lax.broadcasted_iota(jnp.int32, (8, ROWS), 0)
    sc1_recv[0] = jnp.where(rows8 == 0, loss, jnp.where(rows8 == 1, slope, 0.0)) * LN2

    def a_copy(k, slot):
        return remote(sc1_recv.at[0], sc1_recv.at[slot], a_ss.at[k], a_rs.at[slot], row_device(k))

    for k in range(1, NB):
        a_copy(k, row_back[k]).start()

    o_copy = remote(sc2_recv.at[0], sc2_recv.at[1], o_ss, o_rs, col_device(0, 1))

    def b_copy(k, slot):
        return remote(sc3_recv.at[0], sc3_recv.at[slot], b_ss.at[k], b_rs.at[slot], col_device(k))

    def sums_over_rows():
        for k in range(1, NB):
            a_copy(0, k).wait_recv()
        sc2_recv[0] = jnp.sum(sc1_recv[...], axis=0)
        o_copy.start()

    def sums_over_columns():
        o_copy.wait_recv()
        sc3_recv[0] = sc2_recv[0] + sc2_recv[1]
        for k in range(1, NJ):
            b_copy(k, col_back[k]).start()

    half_scale = 0.5 * scale4
    CHUNK = 16

    def s_copy(k):
        return remote(
            sib_send.at[k], sib_recv.at[k], s_ss.at[k], s_rs.at[k], col_device(0, 1)
        )

    class Scatter:
        def __init__(self, places, back, device, part, send, mid, recv, ss, ms, rs):
            self.places, self.back, self.device, self.part = places, back, device, part
            self.out, self.mid, self.recv = send, mid, recv
            self.ss, self.ms, self.rs = ss, ms, rs
            self.size = send.shape[1] // 2

        def half(self, ref, k, h):
            return ref.at[k] if h is None else ref.at[k, pl.ds(h * self.size, self.size)]

        def rows(self, h):
            return slice(h * self.size, (h + 1) * self.size)

        def over(self, k, h, slot, to):
            sem = self.rs.at[slot, h or 0]
            return remote(
                self.half(self.out, k, h),
                self.half(self.recv, slot, h),
                self.ss.at[k, h or 0],
                sem,
                self.device(to),
            )

        def by_way(self, k, h, slot, to):
            return remote(
                self.half(self.out, k, h),
                self.mid.at[slot],
                self.ss.at[k, h],
                self.ms.at[slot],
                self.device(to),
            )

        def sends(self, k):
            step, far = self.places[k]
            if step and far:
                ring = self.places.index((step, 0))
                return [self.by_way(k, 0, ring, 1), self.by_way(k, 1, self.back[k], ring)]
            if far:
                return [self.over(k, 0, 1, 1), self.over(k, 1, 1, 1)]
            return [self.over(k, None, self.back[k], k)] if step else []

        def emit(self, k):
            step, far = self.places[k]
            block = self.part[k]
            if k == 0:
                return
            if step and not far:
                self.by_way(0, 0, k, 1).wait_recv()
                self.out[k, self.rows(0)] = (
                    block[self.rows(0)] + self.mid[k].astype(F32)
                ).astype(BF16)
                self.out[k, self.rows(1)] = block[self.rows(1)].astype(BF16)
            elif step:
                self.out[k] = block.astype(BF16)
            else:
                self.out[k, self.rows(0)] = block[self.rows(0)].astype(BF16)
            for copy in self.sends(k) if step else [self.over(k, 0, 1, 1)]:
                copy.start()

        def last(self):
            total = self.part[1, self.rows(1)]
            for k, (step, far) in enumerate(self.places):
                if step and far:
                    self.by_way(0, 0, k, 1).wait_recv()
                    total = total + self.mid[k].astype(F32)
            self.out[1, self.rows(1)] = total.astype(BF16)
            self.over(1, 1, 1, 1).start()

        def result(self):
            total = self.part[0]
            for k, (step, far) in enumerate(self.places):
                if step and not far:
                    self.over(0, None, k, k).wait_recv()
                    total = total + self.recv[k].astype(F32)
            for h in range(2):
                self.over(0, h, 1, 1).wait_recv()
            return total + self.recv[1].astype(F32)

        def drain(self):
            for k in range(len(self.places)):
                for copy in self.sends(k):
                    copy.wait_send()

    events_out = Scatter(
        row_places, row_back, row_device, de_part, de_send, de_mid, de_recv, de_ss, de_ms, de_rs
    )
    images_out = Scatter(
        col_places, col_back, col_device, own_part, di_send, di_mid, di_recv, di_ss, di_ms, di_rs
    )

    def weights(tr, tc):
        lse = cl[tc]
        for c in range(PAIR // CHUNK):
            at = pl.ds(tr * PAIR + c * CHUNK, CHUNK)
            v = lg[tc, at]
            row = rl[at]
            g = jnp.exp2(v - jnp.concatenate([row] * 4, axis=1)) + jnp.exp2(v - lse)
            wt[tc, at] = (g * half_scale).astype(BF16)
        return 0

    def pass_on(t):
        for k in (2 * t + 1, 2 * t):
            s_copy(k).wait_recv()
            own_part[k] = own_part[k] + sib_recv[k].astype(F32)
            images_out.emit(k)

    def column_weights(t):
        for u in range(min(t + 1, Y)):
            weights(u, t)
        if t == 0:
            v = lg[0, 0:ROWS, 0:ROWS]
            g = jnp.exp2(v - rl[0:ROWS]) + jnp.exp2(v - cl[0, :, 0:ROWS])
            wt[0, 0:ROWS, 0:ROWS] = (
                jnp.where(eye, g - 2.0, g) * half_scale[:, :ROWS]
            ).astype(BF16)

    def row_weights(t):
        for u in range(min(t, X)):
            weights(t, u)

    for t in reversed(range(STEPS)):
        if t == STEPS - 1 and t < X:
            column_weights(t)
        if t < X:
            part = dot(et_all[...], wt[t])
        if t < Y:
            row_weights(t)
        if t < X:
            for f in range(2):
                sib_send[2 * t + f] = part[:, (2 * f + 1) * ROWS : (2 * f + 2) * ROWS].astype(BF16)
                own_part[2 * t + f] = part[:, 2 * f * ROWS : (2 * f + 1) * ROWS]
            for f in range(2):
                s_copy(2 * t + f).start()
        if t < Y:
            at = slice(t * PAIR, (t + 1) * PAIR)
            total = total_of(
                [
                    dot(wt[j, at], i_all[2 * j : 2 * j + 2].reshape(QUAD, D))
                    for j in range(X)
                ]
            )
        if 0 < t <= X:
            column_weights(t - 1)
        if t < Y:
            de_part[2 * t : 2 * t + 2] = total.reshape(2, ROWS, D)
            for k in (2 * t + 1, 2 * t):
                events_out.emit(k)
        if t < X:
            pass_on(t)
        if t == min(2, STEPS - 1):
            sums_over_rows()
        if t == min(1, STEPS - 1):
            sums_over_columns()

    events_out.last()
    images_out.last()
    for k in range(1, NB):
        r_copy(k, row_back[k]).wait_send()
        a_copy(k, row_back[k]).wait_send()
    for k in range(NJ):
        s_copy(k).wait_send()
        if k > 0:
            b_copy(k, col_back[k]).wait_send()
    for r in range(2):
        for k in range(1 - r, NJ):
            c_copy(k, r, col_back[k] + r * NJ).wait_send()
    o_copy.wait_send()

    def finish(field_ref, inv, direction, place):
        unit = field_ref[...] * inv
        grads_ref[place] = inv * (
            direction - unit * jnp.sum(unit * direction, axis=1, keepdims=True)
        )

    finish(im_ref, inv_i, images_out.result().T, 1)
    finish(ev_ref, inv_e, events_out.result(), 0)
    for k in range(1, NJ):
        b_copy(0, k).wait_recv()
    sums_ref[...] = jnp.sum(sc3_recv[...], axis=0) * (1.0 / (NB * NJ * 2 * ROWS))
    events_out.drain()
    images_out.drain()


def write(grads_ref, sums_ref, eg_hbm, ig_hbm, loss_hbm, sg_hbm, loss_ref, sg_ref, sems):
    copies = [
        pltpu.make_async_copy(grads_ref.at[0], eg_hbm, sems.at[0]),
        pltpu.make_async_copy(grads_ref.at[1], ig_hbm, sems.at[1]),
        pltpu.make_async_copy(loss_ref, loss_hbm, sems.at[2]),
        pltpu.make_async_copy(sg_ref, sg_hbm, sems.at[3]),
    ]
    for copy in copies[:2]:
        copy.start()
    loss_ref[0] = jnp.sum(sums_ref[0:1])
    sg_ref[0] = jnp.sum(sums_ref[1:2])
    for copy in copies[2:]:
        copy.start()
    for copy in copies:
        copy.wait()


def solution(mesh):
    X, Y = mesh.shape["dx"] // 4, mesh.shape["dy"] // 2
    NB, NJ = 2 * Y, 2 * X

    def on_device(events, images, log_scale):
        rows, D = events.shape
        dma = pltpu.SemaphoreType.DMA
        vmem = pl.BlockSpec(memory_space=pltpu.VMEM)
        hbm = pl.BlockSpec(memory_space=pltpu.HBM)
        block = jax.ShapeDtypeStruct((rows, D), F32)
        scalar = jax.ShapeDtypeStruct((1,), F32)
        V = pltpu.VMEM
        grads, sums = pl.pallas_call(
            functools.partial(kernel, X, Y),
            out_shape=(
                jax.ShapeDtypeStruct((2, rows, D), F32),
                jax.ShapeDtypeStruct((8, ROWS), F32),
            ),
            in_specs=[hbm, hbm, hbm],
            out_specs=(vmem, vmem),
            scratch_shapes=[
                V((rows, D), F32),
                V((rows, D), F32),
                pltpu.SMEM((1,), F32),
                V((NB, ROWS, D), BF16),
                V((D, NB * ROWS), BF16),
                V((NJ, 2 * ROWS, D), BF16),
                V((X, D, 4 * ROWS), BF16),
                V((X, NB * ROWS, 4 * ROWS), F32),
                V((X, NB * ROWS, 4 * ROWS), BF16),
                V((NB * ROWS, ROWS), F32),
                V((NB * ROWS, ROWS), F32),
                V((NB * ROWS, ROWS), F32),
                V((X, 8, 4 * ROWS), F32),
                V((X, 8, 4 * ROWS), F32),
                V((X, 8, 4 * ROWS), F32),
                V((NB * ROWS, ROWS), F32),
                V((X, 1, 4 * ROWS), F32),
                V((4, max(NB, 2 * NJ), ROWS), F32),
                V((NB, 2 * NB, ROWS), F32),
                V((4 * NJ, ROWS), F32),
                V((2 * NJ, 4 * NJ, ROWS), F32),
                V((NJ, D, ROWS), BF16),
                V((NJ, D, ROWS), BF16),
                V((NJ, D, ROWS), F32),
                V((NJ, D, ROWS), BF16),
                V((NJ, D // 2, ROWS), BF16),
                V((NJ, D, ROWS), BF16),
                V((NB, ROWS, D), F32),
                V((NB, ROWS, D), BF16),
                V((NB, ROWS // 2, D), BF16),
                V((NB, ROWS, D), BF16),
                V((NB, 8, ROWS), F32),
                V((2, 8, ROWS), F32),
                V((NJ, 8, ROWS), F32),
                dma((3,)),
                dma((3 * NB,)),
                dma((NB, 2)),
                dma((3 * NJ,)),
                dma((NJ, 2)),
                dma((NJ,)),
                dma((NJ,)),
                dma((NB,)),
                dma((NB,)),
                dma((2, NJ)),
                dma((2 * NJ,)),
                dma((NJ,)),
                dma((NJ,)),
                dma((NJ, 2)),
                dma((NJ,)),
                dma((NJ, 2)),
                dma((NB, 2)),
                dma((NB,)),
                dma((NB, 2)),
                dma((NB,)),
                dma((NB,)),
                dma((NJ,)),
                dma((NJ,)),
                dma(()),
                dma(()),
            ],
            compiler_params=pltpu.CompilerParams(
                collective_id=0,
                has_side_effects=True,
                vmem_limit_bytes=60 * 1024 * 1024,
            ),
        )(events, images, log_scale)
        return pl.pallas_call(
            write,
            out_shape=(block, block, scalar, scalar),
            in_specs=[vmem, vmem],
            out_specs=(hbm, hbm, hbm, hbm),
            scratch_shapes=[pltpu.SMEM((1,), F32), pltpu.SMEM((1,), F32), dma((4,))],
        )(grads, sums)

    return jax.shard_map(
        on_device,
        mesh=mesh,
        in_specs=(P(("dx", "dy"), None), P(("dx", "dy"), None), P()),
        out_specs=(P(("dx", "dy"), None), P(("dx", "dy"), None), P(), P()),
        check_vma=False,
    )
```

```python
import functools

import jax
import jax.numpy as jnp
from jax import lax
from jax.experimental import pallas as pl
from jax.experimental.pallas import tpu as pltpu
from jax.sharding import PartitionSpec as P

EPSILON = 1e-06
MESH = pl.DeviceIdType.MESH
LOG2E = 1.4426950408889634
LN2 = 0.6931471805599453
ROWS = 128
GATHER_CUT = 80
SCATTER_CUT = 32
F32 = jnp.float32
BF16 = jnp.bfloat16


def members(n):
    ring = [s for s in (1, n - 1, 2) if 0 < s < n]
    ring = list(dict.fromkeys(ring))
    places = [(0, 0), (0, 1)] + [(s, 0) for s in ring] + [(s, 1) for s in ring]
    back = [places.index((-s % n, f)) for s, f in places]
    return places, back


def dot(a, b):
    return lax.dot_general(a, b, (((1,), (0,)), ((), ())), preferred_element_type=F32)


def kernel(
    X,
    Y,
    ev_hbm,
    im_hbm,
    ls_hbm,
    grads_ref,
    sums_ref,
    ev_ref,
    im_ref,
    ls_ref,
    e_all,
    et_all,
    i_all,
    it_all,
    lg,
    wt,
    rm,
    rs,
    ru,
    cm,
    cs,
    cu,
    rl,
    cl,
    lanes_ref,
    row_recv,
    col_b,
    col_sib,
    col_recv,
    sib_send,
    sib_recv,
    own_part,
    di_send,
    di_mid,
    di_recv,
    de_part,
    de_send,
    de_mid,
    de_recv,
    sc1_recv,
    sc2_recv,
    sc3_recv,
    in_s,
    e_ss,
    e_rs,
    i_ss,
    i_rs,
    f_ss,
    f_rs,
    r_ss,
    r_rs,
    c_ss,
    c_rs,
    s_ss,
    s_rs,
    di_ss,
    di_ms,
    di_rs,
    de_ss,
    de_ms,
    de_rs,
    a_ss,
    a_rs,
    b_ss,
    b_rs,
    o_ss,
    o_rs,
    h_ss,
    h_rs,
):
    NB, NJ = 2 * Y, 2 * X
    STEPS = max(X, Y)
    D = ev_ref.shape[1]
    PAIR, QUAD = 2 * ROWS, 4 * ROWS
    dx, dy = lax.axis_index("dx"), lax.axis_index("dy")
    core, zl, x = dx % 2, (dx // 2) % 2, dx // 4
    y, zh = dy % Y, dy // Y
    row_places, row_back = members(Y)
    col_places, col_back = members(X)

    def row_device(k):
        s, f = row_places[k]
        return ((x * 2 + (zl ^ f)) * 2 + core, zh * Y + (y + s) % Y)

    def row_number(k):
        s, f = row_places[k]
        return (y + s) % Y * 2 + (zl ^ f)

    def col_device(k, r=0):
        s, f = col_places[k]
        return (((x + s) % X * 2 + (zl ^ f)) * 2 + (core ^ r), (zh ^ f) * Y + y)

    def col_number(k):
        s, f = col_places[k]
        return (x + s) % X * 2 + (zh ^ f)

    def remote(src, dst, ss, rsem, device):
        return pltpu.make_async_remote_copy(
            src_ref=src,
            dst_ref=dst,
            send_sem=ss,
            recv_sem=rsem,
            device_id=device,
            device_id_type=MESH,
        )

    loads = [
        pltpu.make_async_copy(ev_hbm, ev_ref, in_s.at[0]),
        pltpu.make_async_copy(im_hbm, im_ref, in_s.at[1]),
        pltpu.make_async_copy(ls_hbm, ls_ref, in_s.at[2]),
    ]
    barrier = pltpu.get_barrier_semaphore()
    partners = [row_device(k) for k in reversed(range(1, NB))]
    partners += [col_device(k) for k in reversed(range(1, NJ))] + [col_device(0, 1)]
    for device in partners:
        pl.semaphore_signal(barrier, inc=1, device_id=device, device_id_type=MESH)
    for load in loads:
        load.start()
    for load in loads:
        load.wait()

    def inverse(ref):
        v = ref[...]
        return lax.rsqrt(jnp.sum(v * v, axis=1, keepdims=True) + EPSILON)

    inv_e, inv_i = inverse(ev_ref), inverse(im_ref)
    e_all[0] = (ev_ref[...] * inv_e).astype(BF16)
    i_all[0, 0:ROWS] = (im_ref[...] * inv_i).astype(BF16)
    scale = jnp.exp(jnp.full((1, ROWS), ls_ref[0], F32))
    scale4 = jnp.concatenate([scale] * 4, axis=1)
    to_base2 = scale4 * LOG2E
    for ref in (rm, cm):
        ref[...] = jnp.full(ref.shape, -1e30, F32)
    for ref in (rs, ru, cs, cu):
        ref[...] = jnp.zeros(ref.shape, F32)

    pl.semaphore_wait(barrier, len(partners))

    sent = []

    def block(ref, k, half):
        return ref.at[k, (pl.ds(0, ROWS), pl.ds(0, GATHER_CUT), pl.ds(GATHER_CUT, ROWS - GATHER_CUT))[half]]

    def e_copy(n, src, dst, half, k):
        sem = e_rs.at[dst, half // 2]
        return remote(block(e_all, src, half), block(e_all, dst, half), e_ss.at[n], sem, row_device(k))

    def i_copy(n, src, dst, half, k):
        sem = i_rs.at[dst, half // 2]
        return remote(block(i_all, src, half), block(i_all, dst, half), i_ss.at[n], sem, col_device(k))

    def f_copy(k):
        half = i_all.at[k, pl.ds(0, ROWS)]
        other = i_all.at[k, pl.ds(ROWS, ROWS)]
        return remote(half, other, f_ss.at[k], f_rs.at[k], col_device(0, 1))

    def send(copy):
        copy.start()
        sent.append(copy)

    def first_sends(k):
        for make, places, back in ((e_copy, row_places, row_back), (i_copy, col_places, col_back)):
            if k < len(places) and places[k][0] * places[k][1] == 0:
                send(make(k, 0, back[k], 0, k))

    def take(make, places, back, k):
        count = len(places)
        step, far = places[k]
        if step and far:
            for half in (1, 2):
                make(0, 0, k, half, k).wait_recv()
        elif k > 0:
            make(0, 0, k, 0, k).wait_recv()
        if far and not step:
            for m in range(2, count):
                if places[m][1] == 0:
                    to = places.index((-places[m][0] % (count // 2), 1))
                    send(make(count + m, 1, to, 1, m))
        elif step and not far:
            send(make(2 * count + k, k, places.index((step, 1)), 2, 1))

    send(f_copy(0))
    for k in range(1, max(NB, NJ)):
        first_sends(k)

    eye = lax.broadcasted_iota(jnp.int32, (ROWS, ROWS), 0) == lax.broadcasted_iota(
        jnp.int32, (ROWS, ROWS), 1
    )

    def to_lanes(column):
        return jnp.sum(jnp.where(eye, column, 0.0), axis=0, keepdims=True)

    def to_rows(lanes):
        return jnp.sum(jnp.where(eye, lanes, 0.0), axis=1, keepdims=True)

    def lanes_of(v):
        return [v[:, ROWS * c : ROWS * (c + 1)] for c in range(v.shape[1] // ROWS)]

    def fold(v, op):
        return op(v.reshape(v.shape[0] // 8, 8, v.shape[1]), axis=0)

    def total_of(terms):
        return functools.reduce(jnp.add, terms)

    def tile(tr, tc):
        at = pl.ds(tr * PAIR, PAIR)
        v = dot(e_all[2 * tr : 2 * tr + 2].reshape(PAIR, D), it_all[tc]) * to_base2
        lg[tc, at] = v
        parts = lanes_of(v)
        old = rm[at]
        new = functools.reduce(jnp.maximum, parts, old)
        terms = [jnp.exp2(p - new) for p in parts]
        keep = jnp.exp2(old - new)
        rs[at] = rs[at] * keep + total_of(terms)
        ru[at] = ru[at] * keep + total_of([e * p for e, p in zip(terms, parts)])
        rm[at] = new
        old = cm[tc]
        new = jnp.maximum(old, fold(v, jnp.max))
        v = v.reshape(PAIR // 8, 8, QUAD)
        terms = jnp.exp2(v - new[None])
        keep = jnp.exp2(old - new)
        cs[tc] = cs[tc] * keep + jnp.sum(terms, axis=0)
        cu[tc] = cu[tc] * keep + jnp.sum(terms * v, axis=0)
        cm[tc] = new

    for t in range(STEPS):
        for k in (2 * t, 2 * t + 1):
            if t < X:
                take(i_copy, col_places, col_back, k)
                if k > 0:
                    send(f_copy(k))
            if t < Y:
                take(e_copy, row_places, row_back, k)
        if t < Y:
            for u in range(min(t, X)):
                tile(t, u)
        if t < X:
            for k in (2 * t, 2 * t + 1):
                f_copy(k).wait_recv()
            it_all[t] = i_all[2 * t : 2 * t + 2].reshape(QUAD, D).T
            for u in range(min(t + 1, Y)):
                tile(u, t)

    def r_copy(k, slot):
        return remote(row_recv.at[0], row_recv.at[slot], r_ss.at[k], r_rs.at[slot], row_device(k))

    def c_copy(k, slot):
        return remote(col_recv.at[0], col_recv.at[slot], c_ss.at[k], c_rs.at[slot], col_device(k))

    def merge(lse, mean):
        top = jnp.max(lse, axis=0)
        share = jnp.exp2(lse - top[None])
        tot = jnp.sum(share, axis=0)
        return top + jnp.log2(tot), jnp.sum(share * mean, axis=0) / tot

    def merge_columns(ref):
        return merge(ref[:, 0 : 2 * NJ], ref[:, 2 * NJ :])

    for t in range(X):
        v = cm[t]
        top = jnp.max(v, axis=0, keepdims=True)
        share = jnp.exp2(v - top)
        tot = jnp.sum(cs[t] * share, axis=0, keepdims=True)
        mean = jnp.sum(cu[t] * share, axis=0, keepdims=True) / tot
        lse = lanes_of(top + jnp.log2(tot))
        mean = lanes_of(mean)
        for c in range(4):
            number = 2 * col_number(2 * t + c // 2)
            col_sib[0, pl.ds(number + c % 2, 1)] = lse[c]
            col_sib[0, pl.ds(2 * NJ + number + c % 2, 1)] = mean[c]
            col_b[pl.ds(number + 1 - c % 2, 1)] = lse[c]
            col_b[pl.ds(2 * NJ + number + 1 - c % 2, 1)] = mean[c]
    h_copy = remote(col_b, col_sib.at[1], h_ss, h_rs, col_device(0, 1))
    h_copy.start()
    for b in range(NB):
        at = pl.ds(b * ROWS, ROWS)
        v = rm[at]
        top = jnp.max(v, axis=1, keepdims=True)
        share = jnp.exp2(v - top)
        tot = jnp.sum(rs[at] * share, axis=1, keepdims=True)
        mean = jnp.sum(ru[at] * share, axis=1, keepdims=True) / tot
        number = row_number(b)
        row_recv[0, pl.ds(number, 1)] = to_lanes(top + jnp.log2(tot))
        row_recv[0, pl.ds(NB + number, 1)] = to_lanes(mean)
    for k in reversed(range(1, NB)):
        r_copy(k, row_back[k]).start()
    h_copy.wait_recv()
    lse, mean = merge_columns(col_sib)
    col_recv[0, 0 : 2 * NJ] = lse
    col_recv[0, 2 * NJ :] = mean
    for k in reversed(range(1, NJ)):
        c_copy(k, col_back[k]).start()
    for t in range(Y):
        et_all[:, t * PAIR : (t + 1) * PAIR] = e_all[2 * t : 2 * t + 2].reshape(PAIR, D).T
    for copy in sent:
        copy.wait_send()
    h_copy.wait_send()
    for k in range(1, NJ):
        c_copy(0, k).wait_recv()
    col_lse, col_mean = merge_columns(col_recv)
    lanes_ref[0, 0 : 2 * NJ] = col_lse
    lanes_ref[1, 0 : 2 * NJ] = col_mean
    own_col = pl.ds(2 * col_number(0), 1)
    own_col_lse, own_col_mean = lanes_ref[0, own_col], lanes_ref[1, own_col]
    for t in range(X):
        cl[t] = jnp.concatenate(
            [
                lanes_ref[0, pl.ds(2 * col_number(2 * t + c // 2) + c % 2, 1)]
                for c in range(4)
            ],
            axis=1,
        )
    for k in range(1, NB):
        r_copy(0, k).wait_recv()
    row_lse, row_mean = merge(row_recv[:, 0:NB], row_recv[:, NB:])
    lanes_ref[2, 0:NB] = row_lse
    lanes_ref[3, 0:NB] = row_mean
    own_row = pl.ds(row_number(0), 1)
    own_row_lse, own_row_mean = lanes_ref[2, own_row], lanes_ref[3, own_row]
    for b in range(NB):
        row = lanes_ref[2, pl.ds(row_number(b), 1)]
        rl[pl.ds(b * ROWS, ROWS)] = jnp.broadcast_to(to_rows(row), (ROWS, ROWS))

    diagonal = jnp.sum(
        jnp.where(eye, lg[0, 0:ROWS, 0:ROWS], 0.0), axis=0, keepdims=True
    )
    loss = 0.5 * (own_row_lse + own_col_lse) - diagonal
    slope = 0.5 * (own_row_mean + own_col_mean) - diagonal
    rows8 = lax.broadcasted_iota(jnp.int32, (8, ROWS), 0)
    sc1_recv[0] = jnp.where(rows8 == 0, loss, jnp.where(rows8 == 1, slope, 0.0)) * LN2

    def a_copy(k, slot):
        return remote(sc1_recv.at[0], sc1_recv.at[slot], a_ss.at[k], a_rs.at[slot], row_device(k))

    o_copy = remote(sc2_recv.at[0], sc2_recv.at[1], o_ss, o_rs, col_device(0, 1))

    def b_copy(k, slot):
        return remote(sc3_recv.at[0], sc3_recv.at[slot], b_ss.at[k], b_rs.at[slot], col_device(k))

    def sums_over_rows():
        for k in range(1, NB):
            a_copy(0, k).wait_recv()
        sc2_recv[0] = jnp.sum(sc1_recv[...], axis=0)
        o_copy.start()

    def sums_over_columns():
        o_copy.wait_recv()
        sc3_recv[0] = sc2_recv[0] + sc2_recv[1]
        for k in range(1, NJ):
            b_copy(k, col_back[k]).start()

    half_scale = 0.5 * scale4
    CHUNK = 16

    def s_copy(k):
        return remote(
            sib_send.at[k], sib_recv.at[k], s_ss.at[k], s_rs.at[k], col_device(0, 1)
        )

    class Scatter:
        def __init__(self, places, back, device, part, send, mid, recv, ss, ms, rs):
            self.places, self.back, self.device, self.part = places, back, device, part
            self.out, self.mid, self.recv = send, mid, recv
            self.ss, self.ms, self.rs = ss, ms, rs
            self.size = send.shape[1]
            self.cut = self.size // ROWS * SCATTER_CUT

        def half(self, ref, k, h):
            if h is None:
                return ref.at[k]
            return ref.at[k, pl.ds(self.cut, self.size - self.cut) if h else pl.ds(0, self.cut)]

        def rows(self, h):
            return slice(self.cut, self.size) if h else slice(0, self.cut)

        def came(self, slot, h):
            return self.mid.at[slot, pl.ds(0, self.size - self.cut if h else self.cut)]

        def over(self, k, h, slot, to):
            sem = self.rs.at[slot, h or 0]
            return remote(
                self.half(self.out, k, h),
                self.half(self.recv, slot, h),
                self.ss.at[k, h or 0],
                sem,
                self.device(to),
            )

        def by_way(self, k, h, slot, to):
            return remote(
                self.half(self.out, k, h),
                self.came(slot, h),
                self.ss.at[k, h],
                self.ms.at[slot],
                self.device(to),
            )

        def sends(self, k):
            step, far = self.places[k]
            if step and far:
                ring = self.places.index((step, 0))
                return [self.by_way(k, 0, ring, 1), self.by_way(k, 1, self.back[k], ring)]
            if far:
                return [self.over(k, 0, 1, 1), self.over(k, 1, 1, 1)]
            return [self.over(k, None, self.back[k], k)] if step else []

        def emit(self, k):
            step, far = self.places[k]
            block = self.part[k]
            if k == 0:
                return
            if step and not far:
                self.by_way(0, 0, k, 1).wait_recv()
                self.out[k, self.rows(0)] = (
                    block[self.rows(0)] + self.came(k, 0)[...].astype(F32)
                ).astype(BF16)
                self.out[k, self.rows(1)] = block[self.rows(1)].astype(BF16)
            elif step:
                self.out[k] = block.astype(BF16)
            else:
                self.out[k, self.rows(0)] = block[self.rows(0)].astype(BF16)
            for copy in self.sends(k) if step else [self.over(k, 0, 1, 1)]:
                copy.start()

        def last(self):
            total = self.part[1, self.rows(1)]
            for k, (step, far) in enumerate(self.places):
                if step and far:
                    self.by_way(0, 1, k, 1).wait_recv()
                    total = total + self.came(k, 1)[...].astype(F32)
            self.out[1, self.rows(1)] = total.astype(BF16)
            self.over(1, 1, 1, 1).start()

        def result(self):
            total = self.part[0]
            for k, (step, far) in enumerate(self.places):
                if step and not far:
                    self.over(0, None, k, k).wait_recv()
                    total = total + self.recv[k].astype(F32)
            for h in range(2):
                self.over(0, h, 1, 1).wait_recv()
            return total + self.recv[1].astype(F32)

        def drain(self):
            for k in range(len(self.places)):
                for copy in self.sends(k):
                    copy.wait_send()

    events_out = Scatter(
        row_places, row_back, row_device, de_part, de_send, de_mid, de_recv, de_ss, de_ms, de_rs
    )
    images_out = Scatter(
        col_places, col_back, col_device, own_part, di_send, di_mid, di_recv, di_ss, di_ms, di_rs
    )

    def weights(tr, tc):
        lse = cl[tc]
        for c in range(PAIR // CHUNK):
            at = pl.ds(tr * PAIR + c * CHUNK, CHUNK)
            v = lg[tc, at]
            row = rl[at]
            g = jnp.exp2(v - jnp.concatenate([row] * 4, axis=1)) + jnp.exp2(v - lse)
            wt[tc, at] = (g * half_scale).astype(BF16)
        return 0

    def pass_on(t):
        for k in (2 * t + 1, 2 * t):
            s_copy(k).wait_recv()
            own_part[k] = own_part[k] + sib_recv[k].astype(F32)
            images_out.emit(k)

    def column_weights(t):
        for u in range(min(t + 1, Y)):
            weights(u, t)
        if t == 0:
            v = lg[0, 0:ROWS, 0:ROWS]
            g = jnp.exp2(v - rl[0:ROWS]) + jnp.exp2(v - cl[0, :, 0:ROWS])
            wt[0, 0:ROWS, 0:ROWS] = (
                jnp.where(eye, g - 2.0, g) * half_scale[:, :ROWS]
            ).astype(BF16)

    def row_weights(t):
        for u in range(min(t, X)):
            weights(t, u)

    for t in reversed(range(STEPS)):
        if t == STEPS - 1 and t < X:
            column_weights(t)
        if t < X:
            part = dot(et_all[...], wt[t])
        if t < Y:
            row_weights(t)
        if t < X:
            for f in range(2):
                sib_send[2 * t + f] = part[:, (2 * f + 1) * ROWS : (2 * f + 2) * ROWS].astype(BF16)
                own_part[2 * t + f] = part[:, 2 * f * ROWS : (2 * f + 1) * ROWS]
            for f in range(2):
                s_copy(2 * t + f).start()
        if t == STEPS - 1:
            for k in range(1, NB):
                a_copy(k, row_back[k]).start()
        if t < Y:
            at = slice(t * PAIR, (t + 1) * PAIR)
            total = total_of(
                [
                    dot(wt[j, at], i_all[2 * j : 2 * j + 2].reshape(QUAD, D))
                    for j in range(X)
                ]
            )
        if 0 < t <= X:
            column_weights(t - 1)
        if t < Y:
            de_part[2 * t : 2 * t + 2] = total.reshape(2, ROWS, D)
            for k in (2 * t + 1, 2 * t):
                events_out.emit(k)
        if t < X:
            pass_on(t)
        if t == min(1, STEPS - 1):
            sums_over_rows()
        if t == 0:
            sums_over_columns()

    events_out.last()
    images_out.last()
    for k in range(1, NB):
        r_copy(k, row_back[k]).wait_send()
        a_copy(k, row_back[k]).wait_send()
    for k in range(NJ):
        s_copy(k).wait_send()
        if k > 0:
            b_copy(k, col_back[k]).wait_send()
            c_copy(k, col_back[k]).wait_send()
    o_copy.wait_send()
    events_out.drain()
    images_out.drain()

    def finish(field_ref, inv, direction, place):
        unit = field_ref[...] * inv
        grads_ref[place] = inv * (
            direction - unit * jnp.sum(unit * direction, axis=1, keepdims=True)
        )

    finish(im_ref, inv_i, images_out.result().T, 1)
    finish(ev_ref, inv_e, events_out.result(), 0)
    for k in range(1, NJ):
        b_copy(0, k).wait_recv()
    sums_ref[...] = jnp.sum(sc3_recv[...], axis=0) * (1.0 / (NB * NJ * 2 * ROWS))


def write(grads_ref, sums_ref, eg_hbm, ig_hbm, loss_hbm, sg_hbm, loss_ref, sg_ref, sems):
    copies = [
        pltpu.make_async_copy(grads_ref.at[0], eg_hbm, sems.at[0]),
        pltpu.make_async_copy(grads_ref.at[1], ig_hbm, sems.at[1]),
        pltpu.make_async_copy(loss_ref, loss_hbm, sems.at[2]),
        pltpu.make_async_copy(sg_ref, sg_hbm, sems.at[3]),
    ]
    for copy in copies[:2]:
        copy.start()
    loss_ref[0] = jnp.sum(sums_ref[0:1])
    sg_ref[0] = jnp.sum(sums_ref[1:2])
    for copy in copies[2:]:
        copy.start()
    for copy in copies:
        copy.wait()


def solution(mesh):
    X, Y = mesh.shape["dx"] // 4, mesh.shape["dy"] // 2
    NB, NJ = 2 * Y, 2 * X

    def on_device(events, images, log_scale):
        rows, D = events.shape
        dma = pltpu.SemaphoreType.DMA
        vmem = pl.BlockSpec(memory_space=pltpu.VMEM)
        hbm = pl.BlockSpec(memory_space=pltpu.HBM)
        block = jax.ShapeDtypeStruct((rows, D), F32)
        scalar = jax.ShapeDtypeStruct((1,), F32)
        V = pltpu.VMEM
        grads, sums = pl.pallas_call(
            functools.partial(kernel, X, Y),
            out_shape=(
                jax.ShapeDtypeStruct((2, rows, D), F32),
                jax.ShapeDtypeStruct((8, ROWS), F32),
            ),
            in_specs=[hbm, hbm, hbm],
            out_specs=(vmem, vmem),
            scratch_shapes=[
                V((rows, D), F32),
                V((rows, D), F32),
                pltpu.SMEM((1,), F32),
                V((NB, ROWS, D), BF16),
                V((D, NB * ROWS), BF16),
                V((NJ, 2 * ROWS, D), BF16),
                V((X, D, 4 * ROWS), BF16),
                V((X, NB * ROWS, 4 * ROWS), F32),
                V((X, NB * ROWS, 4 * ROWS), BF16),
                V((NB * ROWS, ROWS), F32),
                V((NB * ROWS, ROWS), F32),
                V((NB * ROWS, ROWS), F32),
                V((X, 8, 4 * ROWS), F32),
                V((X, 8, 4 * ROWS), F32),
                V((X, 8, 4 * ROWS), F32),
                V((NB * ROWS, ROWS), F32),
                V((X, 1, 4 * ROWS), F32),
                V((4, max(NB, 2 * NJ), ROWS), F32),
                V((NB, 2 * NB, ROWS), F32),
                V((4 * NJ, ROWS), F32),
                V((2, 4 * NJ, ROWS), F32),
                V((NJ, 4 * NJ, ROWS), F32),
                V((NJ, D, ROWS), BF16),
                V((NJ, D, ROWS), BF16),
                V((NJ, D, ROWS), F32),
                V((NJ, D, ROWS), BF16),
                V((NJ, D, ROWS), BF16),
                V((NJ, D, ROWS), BF16),
                V((NB, ROWS, D), F32),
                V((NB, ROWS, D), BF16),
                V((NB, ROWS, D), BF16),
                V((NB, ROWS, D), BF16),
                V((NB, 8, ROWS), F32),
                V((2, 8, ROWS), F32),
                V((NJ, 8, ROWS), F32),
                dma((3,)),
                dma((3 * NB,)),
                dma((NB, 2)),
                dma((3 * NJ,)),
                dma((NJ, 2)),
                dma((NJ,)),
                dma((NJ,)),
                dma((NB,)),
                dma((NB,)),
                dma((NJ,)),
                dma((NJ,)),
                dma((NJ,)),
                dma((NJ,)),
                dma((NJ, 2)),
                dma((NJ,)),
                dma((NJ, 2)),
                dma((NB, 2)),
                dma((NB,)),
                dma((NB, 2)),
                dma((NB,)),
                dma((NB,)),
                dma((NJ,)),
                dma((NJ,)),
                dma(()),
                dma(()),
                dma(()),
                dma(()),
            ],
            compiler_params=pltpu.CompilerParams(
                collective_id=0,
                has_side_effects=True,
                vmem_limit_bytes=60 * 1024 * 1024,
            ),
        )(events, images, log_scale)
        return pl.pallas_call(
            write,
            out_shape=(block, block, scalar, scalar),
            in_specs=[vmem, vmem],
            out_specs=(hbm, hbm, hbm, hbm),
            scratch_shapes=[pltpu.SMEM((1,), F32), pltpu.SMEM((1,), F32), dma((4,))],
        )(grads, sums)

    return jax.shard_map(
        on_device,
        mesh=mesh,
        in_specs=(P(("dx", "dy"), None), P(("dx", "dy"), None), P()),
        out_specs=(P(("dx", "dy"), None), P(("dx", "dy"), None), P(), P()),
        check_vma=False,
    )
```

```python
import functools

import jax
import jax.numpy as jnp
from jax import lax
from jax.experimental import pallas as pl
from jax.experimental.pallas import tpu as pltpu
from jax.sharding import PartitionSpec as P

EPSILON = 1e-06
MESH = pl.DeviceIdType.MESH
LOG2E = 1.4426950408889634
LN2 = 0.6931471805599453
ROWS = 128
GATHER_CUT = 80
SCATTER_CUT = 32
F32 = jnp.float32
BF16 = jnp.bfloat16


def members(n):
    ring = [s for s in (1, n - 1, 2) if 0 < s < n]
    ring = list(dict.fromkeys(ring))
    places = [(0, 0), (0, 1)] + [(s, 0) for s in ring] + [(s, 1) for s in ring]
    back = [places.index((-s % n, f)) for s, f in places]
    return places, back


def dot(a, b):
    return lax.dot_general(a, b, (((1,), (0,)), ((), ())), preferred_element_type=F32)


def kernel(
    X,
    Y,
    ev_hbm,
    im_hbm,
    ls_hbm,
    grads_ref,
    sums_ref,
    ev_ref,
    im_ref,
    ls_ref,
    e_all,
    et_all,
    i_all,
    it_all,
    lg,
    wt,
    rm,
    rs,
    ru,
    cm,
    cs,
    cu,
    rl,
    cl,
    lanes_ref,
    row_recv,
    col_b,
    col_sib,
    col_recv,
    sib_send,
    sib_recv,
    own_part,
    di_send,
    di_mid,
    di_recv,
    de_part,
    de_send,
    de_mid,
    de_recv,
    sc1_recv,
    sc2_recv,
    sc3_recv,
    in_s,
    e_ss,
    e_rs,
    i_ss,
    i_rs,
    f_ss,
    f_rs,
    r_ss,
    r_rs,
    c_ss,
    c_rs,
    s_ss,
    s_rs,
    di_ss,
    di_ms,
    di_rs,
    de_ss,
    de_ms,
    de_rs,
    a_ss,
    a_rs,
    b_ss,
    b_rs,
    o_ss,
    o_rs,
    h_ss,
    h_rs,
):
    NB, NJ = 2 * Y, 2 * X
    STEPS = max(X, Y)
    D = ev_ref.shape[1]
    PAIR, QUAD = 2 * ROWS, 4 * ROWS
    dx, dy = lax.axis_index("dx"), lax.axis_index("dy")
    core, zl, x = dx % 2, (dx // 2) % 2, dx // 4
    y, zh = dy % Y, dy // Y
    row_places, row_back = members(Y)
    col_places, col_back = members(X)

    def row_device(k):
        s, f = row_places[k]
        return ((x * 2 + (zl ^ f)) * 2 + core, zh * Y + (y + s) % Y)

    def row_number(k):
        s, f = row_places[k]
        return (y + s) % Y * 2 + (zl ^ f)

    def col_device(k, r=0):
        s, f = col_places[k]
        return (((x + s) % X * 2 + (zl ^ f)) * 2 + (core ^ r), (zh ^ f) * Y + y)

    def col_number(k):
        s, f = col_places[k]
        return (x + s) % X * 2 + (zh ^ f)

    def remote(src, dst, ss, rsem, device):
        return pltpu.make_async_remote_copy(
            src_ref=src,
            dst_ref=dst,
            send_sem=ss,
            recv_sem=rsem,
            device_id=device,
            device_id_type=MESH,
        )

    loads = [
        pltpu.make_async_copy(ev_hbm, ev_ref, in_s.at[0]),
        pltpu.make_async_copy(im_hbm, im_ref, in_s.at[1]),
        pltpu.make_async_copy(ls_hbm, ls_ref, in_s.at[2]),
    ]
    barrier = pltpu.get_barrier_semaphore()
    partners = [row_device(k) for k in reversed(range(1, NB))]
    partners += [col_device(k) for k in reversed(range(1, NJ))] + [col_device(0, 1)]
    for device in partners:
        pl.semaphore_signal(barrier, inc=1, device_id=device, device_id_type=MESH)
    for load in loads:
        load.start()
    for load in loads:
        load.wait()

    def inverse(ref):
        v = ref[...]
        return lax.rsqrt(jnp.sum(v * v, axis=1, keepdims=True) + EPSILON)

    inv_e, inv_i = inverse(ev_ref), inverse(im_ref)
    ev_ref[...] = ev_ref[...] * inv_e
    im_ref[...] = im_ref[...] * inv_i
    e_all[0] = ev_ref[...].astype(BF16)
    i_all[0, 0:ROWS] = im_ref[...].astype(BF16)
    scale = jnp.exp(jnp.full((1, ROWS), ls_ref[0], F32))
    scale4 = jnp.concatenate([scale] * 4, axis=1)
    to_base2 = scale4 * LOG2E
    for ref in (rm, cm):
        ref[...] = jnp.full(ref.shape, -1e30, F32)
    for ref in (rs, ru, cs, cu):
        ref[...] = jnp.zeros(ref.shape, F32)

    pl.semaphore_wait(barrier, len(partners))

    sent = []

    def block(ref, k, half):
        return ref.at[k, (pl.ds(0, ROWS), pl.ds(0, GATHER_CUT), pl.ds(GATHER_CUT, ROWS - GATHER_CUT))[half]]

    def e_copy(n, src, dst, half, k):
        sem = e_rs.at[dst, half // 2]
        return remote(block(e_all, src, half), block(e_all, dst, half), e_ss.at[n], sem, row_device(k))

    def i_copy(n, src, dst, half, k):
        sem = i_rs.at[dst, half // 2]
        return remote(block(i_all, src, half), block(i_all, dst, half), i_ss.at[n], sem, col_device(k))

    def f_copy(k):
        half = i_all.at[k, pl.ds(0, ROWS)]
        other = i_all.at[k, pl.ds(ROWS, ROWS)]
        return remote(half, other, f_ss.at[k], f_rs.at[k], col_device(0, 1))

    def send(copy):
        copy.start()
        sent.append(copy)

    def first_sends(k):
        for make, places, back in ((e_copy, row_places, row_back), (i_copy, col_places, col_back)):
            if k < len(places) and places[k][0] * places[k][1] == 0:
                send(make(k, 0, back[k], 0, k))

    def take(make, places, back, k):
        count = len(places)
        step, far = places[k]
        if step and far:
            for half in (1, 2):
                make(0, 0, k, half, k).wait_recv()
        elif k > 0:
            make(0, 0, k, 0, k).wait_recv()
        if far and not step:
            for m in range(2, count):
                if places[m][1] == 0:
                    to = places.index((-places[m][0] % (count // 2), 1))
                    send(make(count + m, 1, to, 1, m))
        elif step and not far:
            send(make(2 * count + k, k, places.index((step, 1)), 2, 1))

    send(f_copy(0))
    for k in range(1, max(NB, NJ)):
        first_sends(k)

    eye = lax.broadcasted_iota(jnp.int32, (ROWS, ROWS), 0) == lax.broadcasted_iota(
        jnp.int32, (ROWS, ROWS), 1
    )

    def to_lanes(column):
        return jnp.sum(jnp.where(eye, column, 0.0), axis=0, keepdims=True)

    def to_rows(lanes):
        return jnp.sum(jnp.where(eye, lanes, 0.0), axis=1, keepdims=True)

    def lanes_of(v):
        return [v[:, ROWS * c : ROWS * (c + 1)] for c in range(v.shape[1] // ROWS)]

    def fold(v, op):
        return op(v.reshape(v.shape[0] // 8, 8, v.shape[1]), axis=0)

    def total_of(terms):
        return functools.reduce(jnp.add, terms)

    def tile(tr, tc):
        at = pl.ds(tr * PAIR, PAIR)
        v = dot(e_all[2 * tr : 2 * tr + 2].reshape(PAIR, D), it_all[tc]) * to_base2
        lg[tc, at] = v
        parts = lanes_of(v)
        old = rm[at]
        new = functools.reduce(jnp.maximum, parts, old)
        terms = [jnp.exp2(p - new) for p in parts]
        keep = jnp.exp2(old - new)
        rs[at] = rs[at] * keep + total_of(terms)
        ru[at] = ru[at] * keep + total_of([e * p for e, p in zip(terms, parts)])
        rm[at] = new
        old = cm[tc]
        new = jnp.maximum(old, fold(v, jnp.max))
        v = v.reshape(PAIR // 8, 8, QUAD)
        terms = jnp.exp2(v - new[None])
        keep = jnp.exp2(old - new)
        cs[tc] = cs[tc] * keep + jnp.sum(terms, axis=0)
        cu[tc] = cu[tc] * keep + jnp.sum(terms * v, axis=0)
        cm[tc] = new

    for t in range(STEPS):
        for k in (2 * t, 2 * t + 1):
            if t < X:
                take(i_copy, col_places, col_back, k)
                if k > 0:
                    send(f_copy(k))
            if t < Y:
                take(e_copy, row_places, row_back, k)
        if t < Y:
            for u in range(min(t, X)):
                tile(t, u)
        if t < X:
            for k in (2 * t, 2 * t + 1):
                f_copy(k).wait_recv()
            it_all[t] = i_all[2 * t : 2 * t + 2].reshape(QUAD, D).T
            for u in range(min(t + 1, Y)):
                tile(u, t)

    def r_copy(k, slot):
        return remote(row_recv.at[0], row_recv.at[slot], r_ss.at[k], r_rs.at[slot], row_device(k))

    def c_copy(k, slot):
        return remote(col_recv.at[0], col_recv.at[slot], c_ss.at[k], c_rs.at[slot], col_device(k))

    def merge(lse, mean):
        top = jnp.max(lse, axis=0)
        share = jnp.exp2(lse - top[None])
        tot = jnp.sum(share, axis=0)
        return top + jnp.log2(tot), jnp.sum(share * mean, axis=0) / tot

    def merge_columns(ref):
        return merge(ref[:, 0 : 2 * NJ], ref[:, 2 * NJ :])

    for t in range(X):
        v = cm[t]
        top = jnp.max(v, axis=0, keepdims=True)
        share = jnp.exp2(v - top)
        tot = jnp.sum(cs[t] * share, axis=0, keepdims=True)
        mean = jnp.sum(cu[t] * share, axis=0, keepdims=True) / tot
        lse = lanes_of(top + jnp.log2(tot))
        mean = lanes_of(mean)
        for c in range(4):
            number = 2 * col_number(2 * t + c // 2)
            col_sib[0, pl.ds(number + c % 2, 1)] = lse[c]
            col_sib[0, pl.ds(2 * NJ + number + c % 2, 1)] = mean[c]
            col_b[pl.ds(number + 1 - c % 2, 1)] = lse[c]
            col_b[pl.ds(2 * NJ + number + 1 - c % 2, 1)] = mean[c]
    h_copy = remote(col_b, col_sib.at[1], h_ss, h_rs, col_device(0, 1))
    h_copy.start()
    for b in range(NB):
        at = pl.ds(b * ROWS, ROWS)
        v = rm[at]
        top = jnp.max(v, axis=1, keepdims=True)
        share = jnp.exp2(v - top)
        tot = jnp.sum(rs[at] * share, axis=1, keepdims=True)
        mean = jnp.sum(ru[at] * share, axis=1, keepdims=True) / tot
        number = row_number(b)
        row_recv[0, pl.ds(number, 1)] = to_lanes(top + jnp.log2(tot))
        row_recv[0, pl.ds(NB + number, 1)] = to_lanes(mean)
    for k in reversed(range(1, NB)):
        r_copy(k, row_back[k]).start()
    h_copy.wait_recv()
    lse, mean = merge_columns(col_sib)
    col_recv[0, 0 : 2 * NJ] = lse
    col_recv[0, 2 * NJ :] = mean
    for k in reversed(range(1, NJ)):
        c_copy(k, col_back[k]).start()
    for t in range(Y):
        et_all[:, t * PAIR : (t + 1) * PAIR] = e_all[2 * t : 2 * t + 2].reshape(PAIR, D).T
    for copy in sent:
        copy.wait_send()
    h_copy.wait_send()
    for k in range(1, NJ):
        c_copy(0, k).wait_recv()
    col_lse, col_mean = merge_columns(col_recv)
    lanes_ref[0, 0 : 2 * NJ] = col_lse
    lanes_ref[1, 0 : 2 * NJ] = col_mean
    own_col = pl.ds(2 * col_number(0), 1)
    own_col_lse, own_col_mean = lanes_ref[0, own_col], lanes_ref[1, own_col]
    for t in range(X):
        cl[t] = jnp.concatenate(
            [
                lanes_ref[0, pl.ds(2 * col_number(2 * t + c // 2) + c % 2, 1)]
                for c in range(4)
            ],
            axis=1,
        )
    for k in range(1, NB):
        r_copy(0, k).wait_recv()
    row_lse, row_mean = merge(row_recv[:, 0:NB], row_recv[:, NB:])
    lanes_ref[2, 0:NB] = row_lse
    lanes_ref[3, 0:NB] = row_mean
    own_row = pl.ds(row_number(0), 1)
    own_row_lse, own_row_mean = lanes_ref[2, own_row], lanes_ref[3, own_row]
    for b in range(NB):
        row = lanes_ref[2, pl.ds(row_number(b), 1)]
        rl[pl.ds(b * ROWS, ROWS)] = jnp.broadcast_to(to_rows(row), (ROWS, ROWS))

    diagonal = jnp.sum(
        jnp.where(eye, lg[0, 0:ROWS, 0:ROWS], 0.0), axis=0, keepdims=True
    )
    loss = 0.5 * (own_row_lse + own_col_lse) - diagonal
    slope = 0.5 * (own_row_mean + own_col_mean) - diagonal
    rows8 = lax.broadcasted_iota(jnp.int32, (8, ROWS), 0)
    sc1_recv[0] = jnp.where(rows8 == 0, loss, jnp.where(rows8 == 1, slope, 0.0)) * LN2

    def a_copy(k, slot):
        return remote(sc1_recv.at[0], sc1_recv.at[slot], a_ss.at[k], a_rs.at[slot], row_device(k))

    o_copy = remote(sc2_recv.at[0], sc2_recv.at[1], o_ss, o_rs, col_device(0, 1))

    def b_copy(k, slot):
        return remote(sc3_recv.at[0], sc3_recv.at[slot], b_ss.at[k], b_rs.at[slot], col_device(k))

    def sums_over_rows():
        for k in range(1, NB):
            a_copy(0, k).wait_recv()
        sc2_recv[0] = jnp.sum(sc1_recv[...], axis=0)
        o_copy.start()

    def sums_over_columns():
        o_copy.wait_recv()
        sc3_recv[0] = sc2_recv[0] + sc2_recv[1]
        for k in range(1, NJ):
            b_copy(k, col_back[k]).start()

    half_scale = 0.5 * scale4
    CHUNK = 16

    def s_copy(k):
        return remote(
            sib_send.at[k], sib_recv.at[k], s_ss.at[k], s_rs.at[k], col_device(0, 1)
        )

    class Scatter:
        def __init__(self, places, back, device, part, send, mid, recv, ss, ms, rs):
            self.places, self.back, self.device, self.part = places, back, device, part
            self.out, self.mid, self.recv = send, mid, recv
            self.ss, self.ms, self.rs = ss, ms, rs
            self.size = send.shape[1]
            self.cut = self.size // ROWS * SCATTER_CUT

        def half(self, ref, k, h):
            if h is None:
                return ref.at[k]
            return ref.at[k, pl.ds(self.cut, self.size - self.cut) if h else pl.ds(0, self.cut)]

        def rows(self, h):
            return slice(self.cut, self.size) if h else slice(0, self.cut)

        def came(self, slot, h):
            return self.mid.at[slot, pl.ds(0, self.size - self.cut if h else self.cut)]

        def over(self, k, h, slot, to):
            sem = self.rs.at[slot, h or 0]
            return remote(
                self.half(self.out, k, h),
                self.half(self.recv, slot, h),
                self.ss.at[k, h or 0],
                sem,
                self.device(to),
            )

        def by_way(self, k, h, slot, to):
            return remote(
                self.half(self.out, k, h),
                self.came(slot, h),
                self.ss.at[k, h],
                self.ms.at[slot],
                self.device(to),
            )

        def sends(self, k):
            step, far = self.places[k]
            if step and far:
                ring = self.places.index((step, 0))
                return [self.by_way(k, 0, ring, 1), self.by_way(k, 1, self.back[k], ring)]
            if far:
                return [self.over(k, 0, 1, 1), self.over(k, 1, 1, 1)]
            return [self.over(k, None, self.back[k], k)] if step else []

        def emit(self, k):
            step, far = self.places[k]
            block = self.part[k]
            if k == 0:
                return
            if step and not far:
                self.by_way(0, 0, k, 1).wait_recv()
                self.out[k, self.rows(0)] = (
                    block[self.rows(0)] + self.came(k, 0)[...].astype(F32)
                ).astype(BF16)
                self.out[k, self.rows(1)] = block[self.rows(1)].astype(BF16)
            elif step:
                self.out[k] = block.astype(BF16)
            else:
                self.out[k, self.rows(0)] = block[self.rows(0)].astype(BF16)
            for copy in self.sends(k) if step else [self.over(k, 0, 1, 1)]:
                copy.start()

        def last(self):
            total = self.part[1, self.rows(1)]
            for k, (step, far) in enumerate(self.places):
                if step and far:
                    self.by_way(0, 1, k, 1).wait_recv()
                    total = total + self.came(k, 1)[...].astype(F32)
            self.out[1, self.rows(1)] = total.astype(BF16)
            self.over(1, 1, 1, 1).start()

        def result(self):
            total = self.part[0]
            for k, (step, far) in enumerate(self.places):
                if step and not far:
                    self.over(0, None, k, k).wait_recv()
                    total = total + self.recv[k].astype(F32)
            for h in range(2):
                self.over(0, h, 1, 1).wait_recv()
            return total + self.recv[1].astype(F32)

        def drain(self):
            for k in range(len(self.places)):
                for copy in self.sends(k):
                    copy.wait_send()

    events_out = Scatter(
        row_places, row_back, row_device, de_part, de_send, de_mid, de_recv, de_ss, de_ms, de_rs
    )
    images_out = Scatter(
        col_places, col_back, col_device, own_part, di_send, di_mid, di_recv, di_ss, di_ms, di_rs
    )

    def weights(tr, tc):
        lse = cl[tc]
        for c in range(PAIR // CHUNK):
            at = pl.ds(tr * PAIR + c * CHUNK, CHUNK)
            v = lg[tc, at]
            row = rl[at]
            g = jnp.exp2(v - jnp.concatenate([row] * 4, axis=1)) + jnp.exp2(v - lse)
            wt[tc, at] = (g * half_scale).astype(BF16)
        return 0

    def pass_on(t):
        for k in (2 * t + 1, 2 * t):
            s_copy(k).wait_recv()
            own_part[k] = own_part[k] + sib_recv[k].astype(F32)
            images_out.emit(k)

    def column_weights(t):
        for u in range(min(t + 1, Y)):
            weights(u, t)
        if t == 0:
            v = lg[0, 0:ROWS, 0:ROWS]
            g = jnp.exp2(v - rl[0:ROWS]) + jnp.exp2(v - cl[0, :, 0:ROWS])
            wt[0, 0:ROWS, 0:ROWS] = (
                jnp.where(eye, g - 2.0, g) * half_scale[:, :ROWS]
            ).astype(BF16)

    def row_weights(t):
        for u in range(min(t, X)):
            weights(t, u)

    for t in reversed(range(STEPS)):
        if t == STEPS - 1 and t < X:
            column_weights(t)
        if t < X:
            part = dot(et_all[...], wt[t])
        if t < Y:
            row_weights(t)
        if t < X:
            for f in range(2):
                sib_send[2 * t + f] = part[:, (2 * f + 1) * ROWS : (2 * f + 2) * ROWS].astype(BF16)
                own_part[2 * t + f] = part[:, 2 * f * ROWS : (2 * f + 1) * ROWS]
            for f in range(2):
                s_copy(2 * t + f).start()
        if t == STEPS - 1:
            for k in range(1, NB):
                a_copy(k, row_back[k]).start()
        if t < Y:
            at = slice(t * PAIR, (t + 1) * PAIR)
            total = total_of(
                [
                    dot(wt[j, at], i_all[2 * j : 2 * j + 2].reshape(QUAD, D))
                    for j in range(X)
                ]
            )
        if 0 < t <= X:
            column_weights(t - 1)
        if t < Y:
            de_part[2 * t : 2 * t + 2] = total.reshape(2, ROWS, D)
            for k in (2 * t + 1, 2 * t):
                events_out.emit(k)
        if t < X:
            pass_on(t)
        if t == min(1, STEPS - 1):
            sums_over_rows()
        if t == 0:
            sums_over_columns()

    events_out.last()
    images_out.last()
    for k in range(1, NB):
        r_copy(k, row_back[k]).wait_send()
        a_copy(k, row_back[k]).wait_send()
    for k in range(NJ):
        s_copy(k).wait_send()
        if k > 0:
            b_copy(k, col_back[k]).wait_send()
            c_copy(k, col_back[k]).wait_send()
    o_copy.wait_send()
    events_out.drain()
    images_out.drain()

    def finish(unit_ref, inv, direction, place):
        unit = unit_ref[...]
        grads_ref[place] = inv * (
            direction - unit * jnp.sum(unit * direction, axis=1, keepdims=True)
        )

    for k in range(1, NJ):
        b_copy(0, k).wait_recv()
    sums_ref[...] = jnp.sum(sc3_recv[...], axis=0) * (1.0 / (NB * NJ * 2 * ROWS))
    finish(im_ref, inv_i, images_out.result().T, 1)
    finish(ev_ref, inv_e, events_out.result(), 0)


def write(grads_ref, sums_ref, eg_hbm, ig_hbm, loss_hbm, sg_hbm, loss_ref, sg_ref, sems):
    copies = [
        pltpu.make_async_copy(grads_ref.at[0], eg_hbm, sems.at[0]),
        pltpu.make_async_copy(grads_ref.at[1], ig_hbm, sems.at[1]),
        pltpu.make_async_copy(loss_ref, loss_hbm, sems.at[2]),
        pltpu.make_async_copy(sg_ref, sg_hbm, sems.at[3]),
    ]
    for copy in copies[:2]:
        copy.start()
    loss_ref[0] = jnp.sum(sums_ref[0:1])
    sg_ref[0] = jnp.sum(sums_ref[1:2])
    for copy in copies[2:]:
        copy.start()
    for copy in copies:
        copy.wait()


def solution(mesh):
    X, Y = mesh.shape["dx"] // 4, mesh.shape["dy"] // 2
    NB, NJ = 2 * Y, 2 * X

    def on_device(events, images, log_scale):
        rows, D = events.shape
        dma = pltpu.SemaphoreType.DMA
        vmem = pl.BlockSpec(memory_space=pltpu.VMEM)
        hbm = pl.BlockSpec(memory_space=pltpu.HBM)
        block = jax.ShapeDtypeStruct((rows, D), F32)
        scalar = jax.ShapeDtypeStruct((1,), F32)
        V = pltpu.VMEM
        grads, sums = pl.pallas_call(
            functools.partial(kernel, X, Y),
            out_shape=(
                jax.ShapeDtypeStruct((2, rows, D), F32),
                jax.ShapeDtypeStruct((8, ROWS), F32),
            ),
            in_specs=[hbm, hbm, hbm],
            out_specs=(vmem, vmem),
            scratch_shapes=[
                V((rows, D), F32),
                V((rows, D), F32),
                pltpu.SMEM((1,), F32),
                V((NB, ROWS, D), BF16),
                V((D, NB * ROWS), BF16),
                V((NJ, 2 * ROWS, D), BF16),
                V((X, D, 4 * ROWS), BF16),
                V((X, NB * ROWS, 4 * ROWS), F32),
                V((X, NB * ROWS, 4 * ROWS), BF16),
                V((NB * ROWS, ROWS), F32),
                V((NB * ROWS, ROWS), F32),
                V((NB * ROWS, ROWS), F32),
                V((X, 8, 4 * ROWS), F32),
                V((X, 8, 4 * ROWS), F32),
                V((X, 8, 4 * ROWS), F32),
                V((NB * ROWS, ROWS), F32),
                V((X, 1, 4 * ROWS), F32),
                V((4, max(NB, 2 * NJ), ROWS), F32),
                V((NB, 2 * NB, ROWS), F32),
                V((4 * NJ, ROWS), F32),
                V((2, 4 * NJ, ROWS), F32),
                V((NJ, 4 * NJ, ROWS), F32),
                V((NJ, D, ROWS), BF16),
                V((NJ, D, ROWS), BF16),
                V((NJ, D, ROWS), F32),
                V((NJ, D, ROWS), BF16),
                V((NJ, D, ROWS), BF16),
                V((NJ, D, ROWS), BF16),
                V((NB, ROWS, D), F32),
                V((NB, ROWS, D), BF16),
                V((NB, ROWS, D), BF16),
                V((NB, ROWS, D), BF16),
                V((NB, 8, ROWS), F32),
                V((2, 8, ROWS), F32),
                V((NJ, 8, ROWS), F32),
                dma((3,)),
                dma((3 * NB,)),
                dma((NB, 2)),
                dma((3 * NJ,)),
                dma((NJ, 2)),
                dma((NJ,)),
                dma((NJ,)),
                dma((NB,)),
                dma((NB,)),
                dma((NJ,)),
                dma((NJ,)),
                dma((NJ,)),
                dma((NJ,)),
                dma((NJ, 2)),
                dma((NJ,)),
                dma((NJ, 2)),
                dma((NB, 2)),
                dma((NB,)),
                dma((NB, 2)),
                dma((NB,)),
                dma((NB,)),
                dma((NJ,)),
                dma((NJ,)),
                dma(()),
                dma(()),
                dma(()),
                dma(()),
            ],
            compiler_params=pltpu.CompilerParams(
                collective_id=0,
                has_side_effects=True,
                vmem_limit_bytes=60 * 1024 * 1024,
            ),
        )(events, images, log_scale)
        return pl.pallas_call(
            write,
            out_shape=(block, block, scalar, scalar),
            in_specs=[vmem, vmem],
            out_specs=(hbm, hbm, hbm, hbm),
            scratch_shapes=[pltpu.SMEM((1,), F32), pltpu.SMEM((1,), F32), dma((4,))],
        )(grads, sums)

    return jax.shard_map(
        on_device,
        mesh=mesh,
        in_specs=(P(("dx", "dy"), None), P(("dx", "dy"), None), P()),
        out_specs=(P(("dx", "dy"), None), P(("dx", "dy"), None), P(), P()),
        check_vma=False,
    )
```
